256 devices in a mesh: th: 16 (over z_hi, y), tw: 16 (over z_lo, x, core).
Axes of the slice: x: 4, y: 4, z: 8 (z_hi: 4, z_lo: 2; z = z_hi * 2 + z_lo), core: 2. Of those that a mesh axis runs over, the one named last changes fastest.
Arguments:
- query_vectors: bfloat16 [2, 128, 128, 1536], P(None, 'th', 'tw'), may hold values from -6 to 6
- key_vectors: bfloat16 [2, 128, 128, 1536], P(None, 'th', 'tw'), may hold values from -6 to 6
- value_vectors: bfloat16 [2, 128, 128, 1536], P(None, 'th', 'tw'), may hold values from -6 to 6
- out_grad: bfloat16 [2, 128, 128, 3072], P(None, 'th', 'tw'), may hold values from -6 to 6
- out_weight: bfloat16 [1536, 3072], P(('th', 'tw')), may hold values from -0.4375 to 0.4375
- window_extent: int32 [2, 12], replicated, may hold values from 0 to 1, as said below
- edge_pad: int32 [2], replicated, may hold values from 1 to 7, as said below
Outputs:
- block_output: bfloat16 [2, 128, 128, 3072], P(None, 'th', 'tw')
- grad_queries: bfloat16 [2, 128, 128, 1536], P(None, 'th', 'tw')
- grad_keys: bfloat16 [2, 128, 128, 1536], P(None, 'th', 'tw')
- grad_values: bfloat16 [2, 128, 128, 1536], P(None, 'th', 'tw')
The draws below stay inside these ranges and needn't reach their ends.
Inputs may be any that keep to these rules, and one draw needn't show every extreme that they name: `window_extent`: in each of the two rows some head has 0 and some head has 1. `edge_pad`: one of the two entries is 7.
All inputs are finite; a program needn't handle non-finite values.
Results may differ from the reference program's by a relative error of at most 0.018.
Values may be sent and summed in bfloat16 or wider, within the bound.
A program may use at most 192 MiB of HBM per device.

```python
import jax
import jax.numpy as jnp
from jax import lax

D = 3072
HD = 128
HEADS = 12
TILE = 8
FRAMES = 2
E = 1536
NH = 128
NW = 128


def aligned_cells(key):
    grid_shape = (FRAMES, NH, NW, HEADS * HD)
    sign_cells = jnp.where(jax.random.normal(jax.random.fold_in(key, 101), grid_shape) >= 0, 3.5, -3.5)
    return sign_cells


def draw_query_vectors(key, part):
    sign_cells = aligned_cells(key)
    key = jax.random.fold_in(key, 1)
    grid_shape = sign_cells.shape
    cells = jnp.clip(jax.random.normal(key, grid_shape), -5.0, 5.0)
    return cells.astype(jnp.bfloat16)


def draw_key_vectors(key, part):
    sign_cells = aligned_cells(key)
    key = jax.random.fold_in(key, 2)
    grid_shape = sign_cells.shape
    cells = jnp.clip(jax.random.normal(key, grid_shape), -5.0, 5.0)
    return cells.astype(jnp.bfloat16)


def draw_window_extent(key, part):
    key = jax.random.fold_in(key, 3)
    key_one, key_two = jax.random.split(key)
    extents = jax.random.randint(key_one, (2, HEADS), 0, 2)
    shuffled = jax.random.permutation(key_two, HEADS)
    extents = extents.at[:, shuffled[0]].set(1)
    extents = extents.at[:, shuffled[1]].set(0)
    return extents.astype(jnp.int32)


def draw_edge_pad(key, part):
    key = jax.random.fold_in(key, 4)
    key_one, key_two = jax.random.split(key)
    full_side = jax.random.randint(key_one, (), 0, 2)
    other_pad = jax.random.randint(key_two, (), 1, 7)
    return jnp.where(jnp.arange(2) == full_side, 7, other_pad).astype(jnp.int32)


def levels(key, shape, pieces, smallest, top_value):
    def one(axis_at, blocks):
        heights = jax.random.uniform(jax.random.fold_in(jax.random.fold_in(key, 6), axis_at), (blocks,), jnp.float32, smallest / len(pieces), top_value / len(pieces))
        return jnp.repeat(jnp.exp(heights), shape[axis_at] // blocks).reshape((-1,) + (1,) * (len(shape) - axis_at - 1))

    level = one(*pieces[0])
    for cut in pieces[1:]:
        level = level * one(*cut)
    return level


def normal_values(key, dims, deviation, bound, cuts=(), held_as=jnp.bfloat16):
    values = jax.random.normal(key, dims, jnp.float32) * deviation
    if len(cuts) > 0:
        values = levels(key, dims, cuts, -0.22, 0.18) * values
    return jnp.clip(values, min=-bound, max=bound).astype(held_as)


def setup_inputs(seed: int = 0) -> dict:
    arg_keys = jax.random.split(jax.random.key(seed), 8)
    query_vectors = draw_query_vectors(jax.random.fold_in(arg_keys[7], 71), 0)
    key_vectors = draw_key_vectors(jax.random.fold_in(arg_keys[7], 71), 0)
    value_vectors = normal_values(arg_keys[2], (FRAMES, NH, NW, E), 1.0, 6.0, ((1, 16), (2, 16)))
    out_grad = normal_values(arg_keys[3], (FRAMES, NH, NW, D), 1.0, 6.0, ((1, 16), (2, 16)))
    out_weight = normal_values(arg_keys[4], (E, D), (E // 8) ** -0.5, 0.4375, ((0, 256),))
    window_extent = draw_window_extent(jax.random.fold_in(arg_keys[7], 71), 0)
    edge_pad = draw_edge_pad(jax.random.fold_in(arg_keys[7], 71), 0)
    return {"query_vectors": query_vectors, "key_vectors": key_vectors, "value_vectors": value_vectors, "out_grad": out_grad, "out_weight": out_weight, "window_extent": window_extent, "edge_pad": edge_pad}


masked_score = -1e30


def window_mask(extent, tile_size, frames):
    offsets = jnp.arange(3 * tile_size, dtype=jnp.int32) // tile_size - 1
    distance = jnp.abs(offsets)
    inside = (distance[None, :, None] <= extent[0][:, None, None]) & (distance[None, None, :] <= extent[1][:, None, None])
    head_count = extent.shape[1]
    inside = jnp.broadcast_to(inside[:, None], (head_count, frames, 3 * tile_size, 3 * tile_size))
    return inside.reshape(head_count, frames * 9 * tile_size * tile_size)


def cell_valid(row_start, col_start, span_cells, frames, limit_rows, limit_cols):
    row_ids = row_start + jnp.arange(span_cells, dtype=jnp.int32)
    col_ids = col_start + jnp.arange(span_cells, dtype=jnp.int32)
    inside = ((row_ids >= 0) & (row_ids < limit_rows))[:, None] & ((col_ids >= 0) & (col_ids < limit_cols))[None, :]
    return jnp.broadcast_to(inside[None], (frames, span_cells, span_cells)).reshape(-1)


def attend(query_heads, key_heads, value_heads, allowed, factor):
    scores = jnp.einsum("qhd,khd->hqk", query_heads.astype(jnp.float32), key_heads.astype(jnp.float32)) * factor
    scores = jnp.where(allowed[:, None, :], scores, masked_score)
    highest = jnp.max(scores, axis=2, keepdims=True)
    raised = jnp.exp(scores - highest)
    summed = jnp.sum(raised, axis=2, keepdims=True)
    log_total = highest + jnp.log(summed)
    probabilities = (raised / summed).astype(jnp.bfloat16)
    attended = jnp.einsum("hqk,khd->qhd", probabilities.astype(jnp.float32), value_heads.astype(jnp.float32))
    return attended.astype(jnp.bfloat16), log_total


def query_grads(query_heads, key_heads, value_heads, d_heads, log_total, correction, allowed, factor):
    scores = jnp.einsum("qhd,khd->hqk", query_heads.astype(jnp.float32), key_heads.astype(jnp.float32)) * factor
    weights = jnp.where(allowed[:, None, :], jnp.exp(scores - log_total), 0.0)
    d_probs = jnp.einsum("qhd,khd->hqk", d_heads.astype(jnp.float32), value_heads.astype(jnp.float32))
    d_scores = (weights * (d_probs - correction)).astype(jnp.bfloat16)
    grads = jnp.einsum("hqk,khd->qhd", d_scores.astype(jnp.float32), key_heads.astype(jnp.float32)) * factor
    return grads.astype(jnp.bfloat16)


def key_grads(query_heads, d_heads, log_total, correction, key_heads, value_heads, allowed, factor):
    scores = jnp.einsum("qhd,khd->hqk", query_heads.astype(jnp.float32), key_heads.astype(jnp.float32)) * factor
    weights = jnp.where(allowed, jnp.exp(scores - log_total), 0.0)
    d_probs = jnp.einsum("qhd,khd->hqk", d_heads.astype(jnp.float32), value_heads.astype(jnp.float32))
    d_scores = (weights * (d_probs - correction)).astype(jnp.bfloat16)
    grad_k = jnp.einsum("hqk,qhd->khd", d_scores.astype(jnp.float32), query_heads.astype(jnp.float32)) * factor
    weights16 = weights.astype(jnp.bfloat16)
    grad_v = jnp.einsum("hqk,qhd->khd", weights16.astype(jnp.float32), d_heads.astype(jnp.float32))
    return grad_k.astype(jnp.bfloat16), grad_v.astype(jnp.bfloat16)


def reference(query_vectors, key_vectors, value_vectors, out_grad, out_weight, window_extent, edge_pad):
    head_count = HEADS
    head_size = HD
    feature_width = head_count * head_size
    factor = head_size ** -0.5
    tiles_w = NW // TILE
    tiles_all = (NH // TILE) * tiles_w
    cells_tile = FRAMES * TILE * TILE
    limit_rows = NH - edge_pad[0]
    limit_cols = NW - edge_pad[1]
    in_window = window_mask(window_extent, TILE, FRAMES)
    anchor = jnp.zeros((), jnp.int32)

    def padded(array):
        return jnp.pad(array, ((0, 0), (TILE, TILE), (TILE, TILE), (0, 0)))

    def own_block(array, row_start, col_start):
        return lax.dynamic_slice(array, (anchor, row_start, col_start, anchor), (FRAMES, TILE, TILE, array.shape[3]))

    def near_block(array, row_start, col_start):
        return lax.dynamic_slice(array, (anchor, row_start, col_start, anchor), (FRAMES, 3 * TILE, 3 * TILE, array.shape[3]))

    def split_heads(block):
        return block.reshape(-1, head_count, head_size)

    def per_head(block):
        return block.reshape(-1, head_count).T[:, :, None]

    def corner(tile_index):
        return (tile_index // tiles_w) * TILE, (tile_index % tiles_w) * TILE

    def untile(stacked, channels):
        shaped = stacked.reshape(NH // TILE, tiles_w, FRAMES, TILE, TILE, channels)
        return shaped.transpose(2, 0, 3, 1, 4, 5).reshape(FRAMES, NH, NW, channels)

    indices = jnp.arange(tiles_all, dtype=jnp.int32)
    key_padded = padded(key_vectors)
    value_padded = padded(value_vectors)

    def forward_tile(tile_index):
        row_start, col_start = corner(tile_index)
        allowed = in_window & cell_valid(row_start - TILE, col_start - TILE, 3 * TILE, FRAMES, limit_rows, limit_cols)[None, :]
        attended, log_total = attend(split_heads(own_block(query_vectors, row_start, col_start)),
                                     split_heads(near_block(key_padded, row_start, col_start)),
                                     split_heads(near_block(value_padded, row_start, col_start)), allowed, factor)
        return attended.reshape(cells_tile, feature_width), log_total[:, :, 0].T

    attended_tiles, total_tiles = lax.map(forward_tile, indices)
    attended = untile(attended_tiles, feature_width)
    log_totals = untile(total_tiles, head_count)
    block_output = jnp.dot(attended.reshape(-1, feature_width), out_weight, preferred_element_type=jnp.float32)
    block_output = block_output.astype(jnp.bfloat16).reshape(FRAMES, NH, NW, D)
    d_attended = jnp.dot(out_grad.reshape(-1, D), out_weight.T, preferred_element_type=jnp.float32)
    d_attended = d_attended.astype(jnp.bfloat16).reshape(FRAMES, NH, NW, feature_width)
    products = attended.astype(jnp.float32) * d_attended.astype(jnp.float32)
    correction = jnp.sum(products.reshape(FRAMES, NH, NW, head_count, head_size), axis=4)
    query_padded = padded(query_vectors)
    d_padded = padded(d_attended)
    total_padded = padded(log_totals)
    correction_padded = padded(correction)

    def backward_tile(tile_index):
        row_start, col_start = corner(tile_index)
        key_allowed = in_window & cell_valid(row_start - TILE, col_start - TILE, 3 * TILE, FRAMES, limit_rows, limit_cols)[None, :]
        grad_q = query_grads(split_heads(own_block(query_vectors, row_start, col_start)),
                             split_heads(near_block(key_padded, row_start, col_start)),
                             split_heads(near_block(value_padded, row_start, col_start)),
                             split_heads(own_block(d_attended, row_start, col_start)),
                             per_head(own_block(log_totals, row_start, col_start)),
                             per_head(own_block(correction, row_start, col_start)), key_allowed, factor)
        query_allowed = in_window[:, :, None] & cell_valid(row_start, col_start, TILE, FRAMES, limit_rows, limit_cols)[None, None, :]
        grad_k, grad_v = key_grads(split_heads(near_block(query_padded, row_start, col_start)),
                                   split_heads(near_block(d_padded, row_start, col_start)),
                                   per_head(near_block(total_padded, row_start, col_start)),
                                   per_head(near_block(correction_padded, row_start, col_start)),
                                   split_heads(own_block(key_vectors, row_start, col_start)),
                                   split_heads(own_block(value_vectors, row_start, col_start)), query_allowed, factor)
        return (grad_q.reshape(cells_tile, feature_width), grad_k.reshape(cells_tile, feature_width),
                grad_v.reshape(cells_tile, feature_width))

    grad_q_tiles, grad_k_tiles, grad_v_tiles = lax.map(backward_tile, indices)
    return (block_output, untile(grad_q_tiles, feature_width), untile(grad_k_tiles, feature_width),
            untile(grad_v_tiles, feature_width))
```

```python
import jax
import jax.numpy as jnp
from jax import lax
from jax.experimental import pallas as pl
from jax.experimental.pallas import tpu as pltpu
from jax.sharding import PartitionSpec as P

MESH = pl.DeviceIdType.MESH
HEADS, HD, TOK = 12, 128, 128
GROUPS, PER = 4, 3
D, E = 3072, 1536
SLABS = 8
SLABW = D // SLABS
OWN = 4
CELLS = 9 * TOK
MASKED = -1e30
FACTOR = HD ** (-0.5)
BF, F32 = jnp.bfloat16, jnp.float32


def nt(a, b):
    return lax.dot_general(a, b, (((1,), (1,)), ((), ())), preferred_element_type=F32)


def nn(a, b):
    return jnp.dot(a, b, preferred_element_type=F32)


def kernel(
    ext_ref, pad_ref, q_hbm, k_hbm, v_hbm, g_hbm, w_hbm,
    out_ref, dq_ref, dk_ref, dv_ref,
    qn, kn, vn, dn, wb, grads, pieces, block, att, probs, own_stats, stats, weights16,
    load_sem, piece_s, piece_r, z_s, z_r, ring_s, ring_r, core_s, core_r, halo_s, halo_r, stat_s, stat_r,
):
    th, tw = lax.axis_index("th"), lax.axis_index("tw")
    zh, y = th // 4, th % 4
    zl, x, core = tw // 8, (tw // 2) % 4, tw % 2
    z = zh * 2 + zl

    def at(zz, yy, xx, cc):
        return ((zz // 2) * 4 + yy, (zz % 2) * 8 + xx * 2 + cc)

    def tile(dr, dc):
        return ((th + dr + 16) % 16, (tw + dc + 16) % 16)

    north, south, west, east = tile(-1, 0), tile(1, 0), tile(0, -1), tile(0, 1)
    y_up, y_down = (y + 1) % 4, (y + 3) % 4
    x_up, x_down = (x + 1) % 4, (x + 3) % 4
    near_xc = [at(z, y, ((x * 2 + core + i) % 8) // 2, (core + i) % 2) for i in range(1, 8)]
    near_z = [at((z + i) % 8, y, x, core) for i in range(1, 8)]
    near_y = [at(z, y_up, x, core), at(z, y_down, x, core)]

    def remote(src, dst, send, recv, device):
        return pltpu.make_async_remote_copy(
            src_ref=src, dst_ref=dst, send_sem=send, recv_sem=recv,
            device_id=device, device_id_type=MESH,
        )

    barrier = pltpu.get_barrier_semaphore()
    greeted = [north, south, west, east] + near_xc + near_z + near_y
    for target in greeted:
        pl.semaphore_signal(barrier, inc=1, device_id=target, device_id_type=MESH)
    loads = []
    for number, (hbm, near) in enumerate(((k_hbm, kn), (v_hbm, vn), (q_hbm, qn))):
        for h in range(HEADS):
            loads.append(pltpu.make_async_copy(
                hbm.at[:, pl.ds(h * HD, HD)], near.at[h, OWN], load_sem.at[number, h]))
    loads.append(pltpu.make_async_copy(g_hbm, grads, load_sem.at[3, 0]))
    mine = x * 2 + core
    slab = core * 4 + x
    loads.append(pltpu.make_async_copy(w_hbm.at[slab], pieces.at[mine], load_sem.at[3, 1]))
    for copy in loads:
        copy.start()
    for copy in loads:
        copy.wait()
    pl.semaphore_wait(barrier, len(greeted))

    nears = (kn, vn, qn, dn)

    def halo(number, g, slot, source, device):
        near = nears[number]
        heads = pl.ds(g * PER, PER)
        return remote(near.at[heads, source], near.at[heads, slot],
                      halo_s.at[number, g, slot], halo_r.at[number, g, slot], device)

    def rows(number, g):
        halo(number, g, 3, OWN, south).start()
        halo(number, g, 5, OWN, north).start()

    def columns(number, g, dr):
        halo(number, g, 1 + dr, OWN + dr, east).start()
        halo(number, g, 7 + dr, OWN + dr, west).start()

    def arrived(number, g, slot):
        halo(number, g, slot, OWN, east).wait_recv()

    def rows_then_columns(number, g):
        arrived(number, g, 3)
        columns(number, g, -1)
        arrived(number, g, 5)
        columns(number, g, 1)

    def all_columns(number, g):
        for slot in (0, 1, 2, 6, 7, 8):
            arrived(number, g, slot)

    for i in range(1, 8):
        t = (mine + i) % 8
        remote(w_hbm.at[(t % 2) * 4 + t // 2], pieces.at[mine], piece_s.at[i - 1], piece_r.at[i - 1],
               near_xc[i - 1]).start()
    for number in (0, 1):
        for g in range(GROUPS):
            rows(number, g)
            columns(number, g, 0)
    for i in range(1, 8):
        remote(w_hbm.at[0], pieces.at[(mine + 8 - i) % 8], piece_s.at[i - 1], piece_r.at[i - 1],
               near_xc[i - 1]).wait_recv()
    block[...] = jnp.concatenate(
        [pieces[t].astype(F32)[0:6] for t in range(8)], axis=0).astype(BF)

    def z_place(zz):
        return wb.at[zz // 2, core, x, y, pl.ds((zz % 2) * 48, 48)]

    own_place = pltpu.make_async_copy(block, z_place(z), load_sem.at[3, 2])
    own_place.start()
    for i in range(1, 8):
        remote(block, z_place(z), z_s.at[i - 1], z_r.at[i - 1], near_z[i - 1]).start()
    own_place.wait()
    for i in range(1, 8):
        remote(block, z_place((z + 8 - i) % 8), z_s.at[i - 1], z_r.at[i - 1], near_z[i - 1]).wait_recv()

    y_dev = (at(z, y_up, x, core), at(z, y_down, x, core))
    x_dev = (at(z, y, x_up, core), at(z, y, x_down, core))
    other = at(z, y, x, 1 - core)
    half = lambda i: pl.ds(i * 2, 2)

    def ring(c, stage):
        along_y = (c % 2 == 0) == (stage == 0)
        if along_y:
            me, devs = y, y_dev
            if stage == 0:
                place = lambda p: wb.at[c, core, x, p]
                part = lambda p, i: wb.at[c, core, x, p, pl.ds(i * 48, 48)]
            else:
                place = lambda p: wb.at[c, core, :, p]
                part = lambda p, i: wb.at[c, core, half(i), p]
        else:
            me, devs = x, x_dev
            if stage == 0:
                place = lambda p: wb.at[c, core, p, y]
                part = lambda p, i: wb.at[c, core, p, y, pl.ds(i * 48, 48)]
            else:
                place = lambda p: wb.at[c, core, p]
                part = lambda p, i: wb.at[c, core, p, half(i)]
        return place, part, me, devs

    def ring_copy(c, stage, i, ref, device):
        return remote(ref, ref, ring_s.at[c, stage, i], ring_r.at[c, stage, i], device)

    def ring_start(c, stage):
        place, part, me, devs = ring(c, stage)
        ring_copy(c, stage, 0, place(me), devs[0]).start()
        ring_copy(c, stage, 1, place(me), devs[1]).start()

    def ring_relay(c, stage):
        place, part, me, devs = ring(c, stage)
        down, up = (me + 3) % 4, (me + 1) % 4
        ring_copy(c, stage, 0, place(down), devs[0]).wait_recv()
        ring_copy(c, stage, 2, part(down, 0), devs[0]).start()
        ring_copy(c, stage, 1, place(up), devs[1]).wait_recv()
        ring_copy(c, stage, 3, part(up, 1), devs[1]).start()
        return place(down), place(up)

    def ring_end(c, stage):
        place, part, me, devs = ring(c, stage)
        far = (me + 2) % 4
        ring_copy(c, stage, 2, part(far, 0), devs[0]).wait_recv()
        ring_copy(c, stage, 3, part(far, 1), devs[1]).wait_recv()
        return place(far)

    def core_copy(c, i):
        place, part, me, devs = ring(c, 1)
        ref = place((me + i) % 4)
        return remote(ref, ref, core_s.at[c, i], core_r.at[c, i], other)

    def core_arrival(c, i):
        along_y = c % 2 == 1
        p = ((y if along_y else x) + i) % 4
        ref = wb.at[c, 1 - core, :, p] if along_y else wb.at[c, 1 - core, p]
        return remote(ref, ref, core_s.at[c, i], core_r.at[c, i], other)

    for c in range(GROUPS):
        ring_start(c, 0)
    for c in range(GROUPS):
        ring_relay(c, 0)
    for c in range(GROUPS):
        ring_end(c, 0)
        ring_start(c, 1)
        core_copy(c, 0).start()
    for c in range(GROUPS):
        ring_relay(c, 1)
        core_copy(c, 1).start()
        core_copy(c, 3).start()
    for g in range(GROUPS):
        rows_then_columns(0, g)
        rows_then_columns(1, g)
    for g in range(GROUPS):
        rows(2, g)
        columns(2, g, 0)
    for c in range(GROUPS):
        ring_end(c, 1)
        core_copy(c, 2).start()
        for i in range(4):
            core_arrival(c, i).wait_recv()
        total = jnp.zeros((TOK, PER * HD), F32)
        for s in range(SLABS):
            w = wb[c, s // 4, s % 4].reshape(PER * HD, SLABW)
            total += nt(grads[:, s * SLABW:(s + 1) * SLABW], w)
        for i in range(PER):
            dn[c * PER + i, OWN] = total[:, i * HD:(i + 1) * HD].astype(BF)
        rows(3, c)
        columns(3, c, 0)

    lane = lax.broadcasted_iota(jnp.int32, (1, CELLS), 1)
    slot, token = lane // TOK, lane % TOK
    dr, dc = slot % 3 - 1, slot // 3 - 1
    row = (th + dr) * 8 + (token // 8) % 8
    col = (tw + dc) * 8 + token % 8
    limit_rows, limit_cols = 128 - pad_ref[0], 128 - pad_ref[1]
    key_ok = (row >= 0) & (row < limit_rows) & (col >= 0) & (col < limit_cols)
    query_ok = (row >= 0) & (row < 128) & (col >= 0) & (col < 128)
    key_bias = jnp.where(key_ok, 0.0, MASKED)
    query_bias = jnp.where(query_ok, 0.0, MASKED)
    far_rows, far_cols = jnp.abs(dr), jnp.abs(dc)

    def window(h, bias):
        inside = (far_rows <= ext_ref[0, h]) & (far_cols <= ext_ref[1, h])
        return jnp.where(inside, bias, MASKED)

    lane_of = lax.broadcasted_iota(jnp.int32, (TOK, TOK), 1)
    for g in range(GROUPS):
        all_columns(0, g)
        all_columns(1, g)

    def forward(g, found):
        for i in range(PER):
            h = g * PER + i
            s = nt(qn[h, OWN], kn[h].reshape(CELLS, HD)) * FACTOR + window(h, key_bias)
            top = jnp.max(s, axis=1, keepdims=True)
            p = jnp.exp(s - top)
            summed = jnp.sum(p, axis=1, keepdims=True)
            w = (p * (1.0 / summed)).astype(BF)
            probs[h] = w
            o = nn(w, vn[h].reshape(CELLS, HD)).astype(BF)
            att[g, :, i * HD:(i + 1) * HD] = o
            correction = jnp.sum(o.astype(F32) * dn[h, OWN].astype(F32), axis=1, keepdims=True)
            found = jnp.where(lane_of == h, top + jnp.log(summed), found)
            found = jnp.where(lane_of == HEADS + h, correction, found)
        return found

    found = lax.fori_loop(0, GROUPS, forward, jnp.zeros((TOK, TOK), F32))
    own_stats[...] = found
    stats[OWN] = found.T

    def stat(slot, source, device):
        return remote(stats.at[source], stats.at[slot], stat_s.at[slot], stat_r.at[slot], device)

    stat(3, OWN, south).start()
    stat(5, OWN, north).start()
    stat(1, OWN, east).start()
    stat(7, OWN, west).start()

    for g in range(GROUPS):
        rows_then_columns(2, g)
        rows_then_columns(3, g)

    for s in range(SLABS):
        total = jnp.zeros((TOK, SLABW), F32)
        for c in range(GROUPS):
            total += nn(att[c], wb[c, s // 4, s % 4].reshape(PER * HD, SLABW))
        out_ref[:, s * SLABW:(s + 1) * SLABW] = total.astype(BF)

    stat(3, OWN, south).wait_recv()
    stat(0, 3, east).start()
    stat(6, 3, west).start()
    stat(5, OWN, north).wait_recv()
    stat(2, 5, east).start()
    stat(8, 5, west).start()

    def query_part(g, carry):
        for i in range(PER):
            h = g * PER + i
            correction = jnp.sum(jnp.where(lane_of == HEADS + h, own_stats[...], 0.0), axis=1, keepdims=True)
            dp = nt(dn[h, OWN], vn[h].reshape(CELLS, HD))
            ds = (probs[h].astype(F32) * (dp - correction)).astype(BF)
            dq = nn(ds, kn[h].reshape(CELLS, HD)) * FACTOR
            dq_ref[:, pl.ds(pl.multiple_of(h * HD, HD), HD)] = dq.astype(BF)
        return carry

    lax.fori_loop(0, GROUPS, query_part, 0)

    for slot in (0, 1, 2, 6, 7, 8):
        stat(slot, OWN, east).wait_recv()
    for g in range(GROUPS):
        all_columns(2, g)
        all_columns(3, g)
    cell = lax.broadcasted_iota(jnp.int32, (TOK, 1), 0)
    own_ok = (th * 8 + (cell // 8) % 8 < limit_rows) & (tw * 8 + cell % 8 < limit_cols)

    def key_part(g, carry):
        for i in range(PER):
            h = g * PER + i
            totals = jnp.concatenate([stats[j, pl.ds(h, 1)] for j in range(9)], axis=1)
            corrections = jnp.concatenate([stats[j, pl.ds(HEADS + h, 1)] for j in range(9)], axis=1)
            shift = window(h, query_bias) - totals
            qs = qn[h].reshape(CELLS, HD)
            ds_near = dn[h].reshape(CELLS, HD)
            w = jnp.exp(nt(kn[h, OWN], qs) * FACTOR + shift)
            dp = nt(vn[h, OWN], ds_near)
            ds = (w * (dp - corrections)).astype(BF)
            dk = jnp.where(own_ok, nn(ds, qs) * FACTOR, 0.0)
            dv = jnp.where(own_ok, nn(w.astype(BF), ds_near), 0.0)
            at_h = pl.ds(pl.multiple_of(h * HD, HD), HD)
            dk_ref[:, at_h] = dk.astype(BF)
            dv_ref[:, at_h] = dv.astype(BF)
        return carry

    lax.fori_loop(0, GROUPS, key_part, 0)

    for i in range(1, 8):
        remote(w_hbm.at[0], pieces.at[0], piece_s.at[i - 1], piece_r.at[i - 1], near_xc[i - 1]).wait_send()
        remote(block, z_place(z), z_s.at[i - 1], z_r.at[i - 1], near_z[i - 1]).wait_send()
    for c in range(GROUPS):
        for stage in range(2):
            place, part, me, devs = ring(c, stage)
            for i in range(2):
                ring_copy(c, stage, i, place(me), devs[i]).wait_send()
                ring_copy(c, stage, 2 + i, part(me, 0), devs[i]).wait_send()
        for i in range(4):
            core_copy(c, i).wait_send()
    for number in range(4):
        for g in range(GROUPS):
            for slot in (0, 1, 2, 3, 5, 6, 7, 8):
                halo(number, g, slot, OWN, east).wait_send()
    for slot in (0, 1, 2, 3, 5, 6, 7, 8):
        stat(slot, OWN, east).wait_send()


def on_device(q, k, v, out_grad, out_weight, extent, pad):
    shape = q.shape
    flat = lambda a: a.reshape(TOK, a.shape[-1])
    pieces = out_weight.reshape(6, SLABS, SLABW).transpose(1, 0, 2)
    pieces = jnp.pad(pieces, ((0, 0), (0, 10), (0, 0)))
    hbm = pl.BlockSpec(memory_space=pl.ANY)
    smem = pl.BlockSpec(memory_space=pltpu.SMEM)
    vmem = pl.BlockSpec(memory_space=pltpu.VMEM)
    near = pltpu.VMEM((HEADS, 9, TOK, HD), BF)
    dma = pltpu.SemaphoreType.DMA
    out, dq, dk, dv = pl.pallas_call(
        kernel,
        out_shape=(
            jax.ShapeDtypeStruct((TOK, D), BF),
            jax.ShapeDtypeStruct((TOK, E), BF),
            jax.ShapeDtypeStruct((TOK, E), BF),
            jax.ShapeDtypeStruct((TOK, E), BF),
        ),
        in_specs=[smem, smem, hbm, hbm, hbm, hbm, vmem],
        out_specs=(vmem, vmem, vmem, vmem),
        scratch_shapes=[
            near, near, near, near,
            pltpu.VMEM((GROUPS, 2, 4, 4, 96, SLABW), BF),
            pltpu.VMEM((TOK, D), BF),
            pltpu.VMEM((8, 16, SLABW), BF),
            pltpu.VMEM((48, SLABW), BF),
            pltpu.VMEM((GROUPS, TOK, PER * HD), BF),
            pltpu.VMEM((HEADS, TOK, CELLS), BF),
            pltpu.VMEM((TOK, TOK), F32),
            pltpu.VMEM((9, TOK, TOK), F32),
            pltpu.VMEM((16, 128), BF),
            dma((4, HEADS)),
            dma((7,)), dma((7,)), dma((7,)), dma((7,)),
            dma((GROUPS, 2, 4)), dma((GROUPS, 2, 4)),
            dma((GROUPS, 4)), dma((GROUPS, 4)),
            dma((4, GROUPS, 9)), dma((4, GROUPS, 9)),
            dma((9,)), dma((9,)),
        ],
        compiler_params=pltpu.CompilerParams(
            collective_id=0, has_side_effects=True, vmem_limit_bytes=60 * 1024 * 1024),
        cost_estimate=pl.CostEstimate(flops=7 * 10**9, bytes_accessed=6 * 10**6, transcendentals=4 * 10**6),
    )(extent, pad, flat(q), flat(k), flat(v), flat(out_grad), pieces)
    return (out.reshape(out_grad.shape), dq.reshape(shape), dk.reshape(shape), dv.reshape(shape))


def solution(mesh):
    cells = P(None, "th", "tw", None)
    return jax.shard_map(
        on_device,
        mesh=mesh,
        in_specs=(cells, cells, cells, cells, P(("th", "tw"), None), P(), P()),
        out_specs=(cells, cells, cells, cells),
        check_vma=False,
    )
```

```python
import jax
import jax.numpy as jnp
from jax import lax
from jax.experimental import pallas as pl
from jax.experimental.pallas import tpu as pltpu
from jax.sharding import PartitionSpec as P

MESH = pl.DeviceIdType.MESH
HEADS, HD, TOK = 12, 128, 128
GROUPS, PER = 4, 3
D, E = 3072, 1536
SLABS = 8
SLABW = D // SLABS
OWN = 4
RELAYED = (2, 3)
ORDER = (2, 3, 0, 1)
Y_FIRST = (1, 3)
CELLS = 9 * TOK
MASKED = -1e30
FACTOR = HD ** (-0.5)
BF, F32 = jnp.bfloat16, jnp.float32


def nt(a, b):
    return lax.dot_general(a, b, (((1,), (1,)), ((), ())), preferred_element_type=F32)


def nn(a, b):
    return jnp.dot(a, b, preferred_element_type=F32)


def kernel(
    ext_ref, pad_ref, q_hbm, k_hbm, v_hbm, g_hbm, w_hbm,
    out_ref, dq_ref, dk_ref, dv_ref,
    qn, kn, vn, dn, wb, grads, pieces, block, att, probs, own_stats, stats, weights16,
    load_sem, piece_s, piece_r, z_s, z_r, ring_s, ring_r, core_s, core_r, halo_s, halo_r, stat_s, stat_r,
    row_relay, col_relay, row_rs, row_rr, col_rs, col_rr,
):
    th, tw = lax.axis_index("th"), lax.axis_index("tw")
    zh, y = th // 4, th % 4
    zl, x, core = tw // 8, (tw // 2) % 4, tw % 2
    z = zh * 2 + zl

    def at(zz, yy, xx, cc):
        return ((zz // 2) * 4 + yy, (zz % 2) * 8 + xx * 2 + cc)

    def tile(dr, dc):
        return ((th + dr + 16) % 16, (tw + dc + 16) % 16)

    north, south, west, east = tile(-1, 0), tile(1, 0), tile(0, -1), tile(0, 1)
    y_up, y_down = (y + 1) % 4, (y + 3) % 4
    x_up, x_down = (x + 1) % 4, (x + 3) % 4
    near_xc = [at(z, y, ((x * 2 + core + i) % 8) // 2, (core + i) % 2) for i in range(1, 8)]
    near_z = [at((z + i) % 8, y, x, core) for i in range(1, 8)]
    near_y = [at(z, y_up, x, core), at(z, y_down, x, core)]

    def remote(src, dst, send, recv, device):
        return pltpu.make_async_remote_copy(
            src_ref=src, dst_ref=dst, send_sem=send, recv_sem=recv,
            device_id=device, device_id_type=MESH,
        )

    barrier = pltpu.get_barrier_semaphore()
    greeted = [north, south, west, east] + near_xc + near_z + near_y
    for target in greeted:
        pl.semaphore_signal(barrier, inc=1, device_id=target, device_id_type=MESH)
    loads = []
    for number, (hbm, near) in enumerate(((k_hbm, kn), (v_hbm, vn), (q_hbm, qn))):
        for h in range(HEADS):
            loads.append(pltpu.make_async_copy(
                hbm.at[:, pl.ds(h * HD, HD)], near.at[h, OWN], load_sem.at[number, h]))
    loads.append(pltpu.make_async_copy(g_hbm, grads, load_sem.at[3, 0]))
    mine = x * 2 + core
    slab = core * 4 + x
    loads.append(pltpu.make_async_copy(w_hbm.at[slab], pieces.at[mine], load_sem.at[3, 1]))
    for copy in loads:
        copy.start()
    for edge, slots in ((tw == 0, (0, 1, 2)), (tw == 15, (6, 7, 8))):
        @pl.when(edge)
        def _():
            for near in (kn, vn, qn, dn):
                for j in slots:
                    near[:, j] = jnp.zeros((HEADS, TOK, HD), BF)
    for copy in loads:
        copy.wait()
    pl.semaphore_wait(barrier, len(greeted))

    nears = (kn, vn, qn, dn)

    def halo(number, g, slot, source, device):
        near = nears[number]
        heads = pl.ds(g * PER, PER)
        return remote(near.at[heads, source], near.at[heads, slot],
                      halo_s.at[number, g, slot], halo_r.at[number, g, slot], device)

    first_row, last_row = y == 0, y == 3
    first_col, last_col = tw == 0, tw == 15
    cross_east, cross_west = tw == 7, tw == 8

    def via(number, g, slot, source, space, send, recv, device):
        return remote(nears[number].at[pl.ds(g * PER, PER), source], space, send, recv, device)

    def rows(number, g):
        if g in RELAYED:
            i = g - RELAYED[0]
            for slot, crossing, straight, device in (
                (3, last_row, south, tile(-3, 0)), (5, first_row, north, tile(3, 0))):
                @pl.when(crossing)
                def _():
                    via(number, g, slot, OWN, row_relay.at[number, i], halo_s.at[number, g, slot],
                        row_rr.at[number, i], device).start()

                @pl.when(jnp.logical_not(crossing))
                def _():
                    halo(number, g, slot, OWN, straight).start()
        else:
            halo(number, g, 3, OWN, south).start()
            halo(number, g, 5, OWN, north).start()

    def row_pass(number, g, slot, device):
        i = g - RELAYED[0]
        return remote(row_relay.at[number, i], nears[number].at[pl.ds(g * PER, PER), slot],
                      row_rs.at[number, i], halo_r.at[number, g, slot], device)

    def pass_rows(number, g):
        if g not in RELAYED:
            return
        i = g - RELAYED[0]
        for slot, crossing, device in ((3, first_row, tile(4, 0)), (5, last_row, tile(-4, 0))):
            @pl.when(crossing)
            def _():
                via(number, g, slot, OWN, row_relay.at[number, i], row_rs.at[number, i],
                    row_rr.at[number, i], north).wait_recv()
                row_pass(number, g, slot, device).start()

    def columns(number, g, dr):
        for slot, crossing, edge, straight, device in (
            (1 + dr, cross_east, last_col, east, tile(0, -7)),
            (7 + dr, cross_west, first_col, west, tile(0, 7))):
            if g in RELAYED:
                i = g - RELAYED[0]

                @pl.when(crossing)
                def _():
                    via(number, g, slot, OWN + dr, col_relay.at[number, i, dr + 1],
                        halo_s.at[number, g, slot], col_rr.at[number, i, dr + 1], device).start()

                @pl.when(jnp.logical_not(crossing | edge))
                def _():
                    halo(number, g, slot, OWN + dr, straight).start()
            else:
                @pl.when(jnp.logical_not(edge))
                def _():
                    halo(number, g, slot, OWN + dr, straight).start()

    def col_pass(number, g, dr, slot, device):
        i = g - RELAYED[0]
        return remote(col_relay.at[number, i, dr + 1], nears[number].at[pl.ds(g * PER, PER), slot],
                      col_rs.at[number, i, dr + 1], halo_r.at[number, g, slot], device)

    def pass_columns(number, g, drs=(0, -1, 1)):
        if g not in RELAYED:
            return
        i = g - RELAYED[0]
        for base, edge, device in ((1, first_col, tile(0, 8)), (7, last_col, tile(0, -8))):
            @pl.when(edge)
            def _():
                for dr in drs:
                    via(number, g, OWN, OWN, col_relay.at[number, i, dr + 1], col_rs.at[number, i, dr + 1],
                        col_rr.at[number, i, dr + 1], north).wait_recv()
                    col_pass(number, g, dr, base + dr, device).start()

    def arrived(number, g, slot):
        halo(number, g, slot, OWN, north).wait_recv()

    def rows_then_columns(number, g):
        arrived(number, g, 3)
        columns(number, g, -1)
        arrived(number, g, 5)
        columns(number, g, 1)

    def all_columns(number, g):
        @pl.when(jnp.logical_not(first_col))
        def _():
            for slot in (0, 1, 2):
                arrived(number, g, slot)

        @pl.when(jnp.logical_not(last_col))
        def _():
            for slot in (6, 7, 8):
                arrived(number, g, slot)

    for i in range(1, 8):
        t = (mine + i) % 8
        remote(w_hbm.at[(t % 2) * 4 + t // 2], pieces.at[mine], piece_s.at[i - 1], piece_r.at[i - 1],
               near_xc[i - 1]).start()
    for number in (0, 1):
        for g in ORDER:
            rows(number, g)
            columns(number, g, 0)
    for i in range(1, 8):
        remote(w_hbm.at[0], pieces.at[(mine + 8 - i) % 8], piece_s.at[i - 1], piece_r.at[i - 1],
               near_xc[i - 1]).wait_recv()
    block[...] = jnp.concatenate(
        [pieces[t].astype(F32)[0:6] for t in range(8)], axis=0).astype(BF)

    def z_place(zz):
        return wb.at[zz // 2, core, x, y, pl.ds((zz % 2) * 48, 48)]

    own_place = pltpu.make_async_copy(block, z_place(z), load_sem.at[3, 2])
    own_place.start()
    for i in range(1, 8):
        remote(block, z_place(z), z_s.at[i - 1], z_r.at[i - 1], near_z[i - 1]).start()
    own_place.wait()
    for number in (0, 1):
        for g in RELAYED:
            pass_rows(number, g)
            pass_columns(number, g, (0,))
    for i in range(1, 8):
        remote(block, z_place((z + 8 - i) % 8), z_s.at[i - 1], z_r.at[i - 1], near_z[i - 1]).wait_recv()

    y_dev = (at(z, y_up, x, core), at(z, y_down, x, core))
    x_dev = (at(z, y, x_up, core), at(z, y, x_down, core))
    other = at(z, y, x, 1 - core)
    half = lambda i: pl.ds(i * 2, 2)

    def ring(c, stage):
        along_y = (c in Y_FIRST) == (stage == 0)
        if along_y:
            me, devs = y, y_dev
            if stage == 0:
                place = lambda p: wb.at[c, core, x, p]
                part = lambda p, i: wb.at[c, core, x, p, pl.ds(i * 48, 48)]
            else:
                place = lambda p: wb.at[c, core, :, p]
                part = lambda p, i: wb.at[c, core, half(i), p]
        else:
            me, devs = x, x_dev
            if stage == 0:
                place = lambda p: wb.at[c, core, p, y]
                part = lambda p, i: wb.at[c, core, p, y, pl.ds(i * 48, 48)]
            else:
                place = lambda p: wb.at[c, core, p]
                part = lambda p, i: wb.at[c, core, p, half(i)]
        return place, part, me, devs

    def ring_copy(c, stage, i, ref, device):
        return remote(ref, ref, ring_s.at[c, stage, i], ring_r.at[c, stage, i], device)

    def ring_start(c, stage):
        place, part, me, devs = ring(c, stage)
        ring_copy(c, stage, 0, place(me), devs[0]).start()
        ring_copy(c, stage, 1, place(me), devs[1]).start()

    def ring_relay(c, stage):
        place, part, me, devs = ring(c, stage)
        down, up = (me + 3) % 4, (me + 1) % 4
        ring_copy(c, stage, 0, place(down), devs[0]).wait_recv()
        ring_copy(c, stage, 2, part(down, 0), devs[0]).start()
        ring_copy(c, stage, 1, place(up), devs[1]).wait_recv()
        ring_copy(c, stage, 3, part(up, 1), devs[1]).start()
        return place(down), place(up)

    def ring_end(c, stage):
        place, part, me, devs = ring(c, stage)
        far = (me + 2) % 4
        ring_copy(c, stage, 2, part(far, 0), devs[0]).wait_recv()
        ring_copy(c, stage, 3, part(far, 1), devs[1]).wait_recv()
        return place(far)

    def core_copy(c, i):
        place, part, me, devs = ring(c, 1)
        ref = place((me + i) % 4)
        return remote(ref, ref, core_s.at[c, i], core_r.at[c, i], other)

    def core_arrival(c, i):
        along_y = c not in Y_FIRST
        p = ((y if along_y else x) + i) % 4
        ref = wb.at[c, 1 - core, :, p] if along_y else wb.at[c, 1 - core, p]
        return remote(ref, ref, core_s.at[c, i], core_r.at[c, i], other)

    for c in range(GROUPS):
        ring_start(c, 0)
    for g in ORDER:
        rows(2, g)
        columns(2, g, 0)
    for c in range(GROUPS):
        ring_relay(c, 0)
    for c in range(GROUPS):
        ring_end(c, 0)
        ring_start(c, 1)
        core_copy(c, 0).start()
    for g in RELAYED:
        pass_rows(2, g)
        pass_columns(2, g, (0,))
    for c in range(GROUPS):
        rows_then_columns(0, c)
        rows_then_columns(1, c)
        ring_relay(c, 1)
        core_copy(c, 1).start()
        core_copy(c, 3).start()
    for c in range(GROUPS):
        ring_end(c, 1)
        core_copy(c, 2).start()
        for i in range(4):
            core_arrival(c, i).wait_recv()
        total = jnp.zeros((TOK, PER * HD), F32)
        for s in range(SLABS):
            w = wb[c, s // 4, s % 4].reshape(PER * HD, SLABW)
            total += nt(grads[:, s * SLABW:(s + 1) * SLABW], w)
        for i in range(PER):
            dn[c * PER + i, OWN] = total[:, i * HD:(i + 1) * HD].astype(BF)
        rows(3, c)
        columns(3, c, 0)
        pass_columns(0, c, (-1, 1))
        pass_columns(1, c, (-1, 1))
        rows_then_columns(2, c)

    lane = lax.broadcasted_iota(jnp.int32, (1, CELLS), 1)
    slot, token = lane // TOK, lane % TOK
    dr, dc = slot % 3 - 1, slot // 3 - 1
    row = (th + dr) * 8 + (token // 8) % 8
    col = (tw + dc) * 8 + token % 8
    limit_rows, limit_cols = 128 - pad_ref[0], 128 - pad_ref[1]
    key_ok = (row >= 0) & (row < limit_rows) & (col >= 0) & (col < limit_cols)
    query_ok = (row >= 0) & (row < 128) & (col >= 0) & (col < 128)
    key_bias = jnp.where(key_ok, 0.0, MASKED)
    query_bias = jnp.where(query_ok, 0.0, MASKED)
    far_rows, far_cols = jnp.abs(dr), jnp.abs(dc)

    def window(h, bias):
        inside = (far_rows <= ext_ref[0, h]) & (far_cols <= ext_ref[1, h])
        return jnp.where(inside, bias, MASKED)

    lane_of = lax.broadcasted_iota(jnp.int32, (TOK, TOK), 1)

    def forward(g, found):
        all_columns(0, g)
        all_columns(1, g)
        for i in range(PER):
            h = g * PER + i
            s = nt(qn[h, OWN], kn[h].reshape(CELLS, HD)) * FACTOR + window(h, key_bias)
            top = jnp.max(s, axis=1, keepdims=True)
            p = jnp.exp(s - top)
            summed = jnp.sum(p, axis=1, keepdims=True)
            w = (p * (1.0 / summed)).astype(BF)
            probs[h] = w
            o = nn(w, vn[h].reshape(CELLS, HD)).astype(BF)
            att[g, :, i * HD:(i + 1) * HD] = o
            correction = jnp.sum(o.astype(F32) * dn[h, OWN].astype(F32), axis=1, keepdims=True)
            found = jnp.where(lane_of == h, top + jnp.log(summed), found)
            found = jnp.where(lane_of == HEADS + h, correction, found)
        return found

    found = lax.fori_loop(0, GROUPS, forward, jnp.zeros((TOK, TOK), F32))
    own_stats[...] = found
    stats[OWN] = found.T

    def stat(slot, source, device):
        return remote(stats.at[source], stats.at[slot], stat_s.at[slot], stat_r.at[slot], device)

    stat(3, OWN, south).start()
    stat(5, OWN, north).start()
    stat(1, OWN, east).start()
    stat(7, OWN, west).start()

    for g in RELAYED:
        pass_rows(3, g)
        pass_columns(3, g, (0,))
        pass_columns(2, g, (-1, 1))
    for g in range(GROUPS):
        rows_then_columns(3, g)

    for s in range(SLABS):
        total = jnp.zeros((TOK, SLABW), F32)
        for c in range(GROUPS):
            total += nn(att[c], wb[c, s // 4, s % 4].reshape(PER * HD, SLABW))
        out_ref[:, s * SLABW:(s + 1) * SLABW] = total.astype(BF)

    stat(3, OWN, south).wait_recv()
    stat(0, 3, east).start()
    stat(6, 3, west).start()
    stat(5, OWN, north).wait_recv()
    stat(2, 5, east).start()
    stat(8, 5, west).start()

    def query_part(g, carry):
        for i in range(PER):
            h = g * PER + i
            correction = jnp.sum(jnp.where(lane_of == HEADS + h, own_stats[...], 0.0), axis=1, keepdims=True)
            dp = nt(dn[h, OWN], vn[h].reshape(CELLS, HD))
            ds = (probs[h].astype(F32) * (dp - correction)).astype(BF)
            dq = nn(ds, kn[h].reshape(CELLS, HD)) * FACTOR
            dq_ref[:, pl.ds(pl.multiple_of(h * HD, HD), HD)] = dq.astype(BF)
        return carry

    lax.fori_loop(0, GROUPS, query_part, 0)

    for g in range(GROUPS):
        pass_columns(3, g, (-1, 1))
    for slot in (0, 1, 2, 6, 7, 8):
        stat(slot, OWN, east).wait_recv()
    cell = lax.broadcasted_iota(jnp.int32, (TOK, 1), 0)
    own_ok = (th * 8 + (cell // 8) % 8 < limit_rows) & (tw * 8 + cell % 8 < limit_cols)

    def key_part(g, carry):
        all_columns(2, g)
        all_columns(3, g)
        for i in range(PER):
            h = g * PER + i
            totals = jnp.concatenate([stats[j, pl.ds(h, 1)] for j in range(9)], axis=1)
            corrections = jnp.concatenate([stats[j, pl.ds(HEADS + h, 1)] for j in range(9)], axis=1)
            shift = window(h, query_bias) - totals
            qs = qn[h].reshape(CELLS, HD)
            ds_near = dn[h].reshape(CELLS, HD)
            w = jnp.exp(nt(kn[h, OWN], qs) * FACTOR + shift)
            dp = nt(vn[h, OWN], ds_near)
            ds = (w * (dp - corrections)).astype(BF)
            dk = jnp.where(own_ok, nn(ds, qs) * FACTOR, 0.0)
            dv = jnp.where(own_ok, nn(w.astype(BF), ds_near), 0.0)
            at_h = pl.ds(pl.multiple_of(h * HD, HD), HD)
            dk_ref[:, at_h] = dk.astype(BF)
            dv_ref[:, at_h] = dv.astype(BF)
        return carry

    lax.fori_loop(0, GROUPS, key_part, 0)

    for i in range(1, 8):
        remote(w_hbm.at[0], pieces.at[0], piece_s.at[i - 1], piece_r.at[i - 1], near_xc[i - 1]).wait_send()
        remote(block, z_place(z), z_s.at[i - 1], z_r.at[i - 1], near_z[i - 1]).wait_send()
    for c in range(GROUPS):
        for stage in range(2):
            place, part, me, devs = ring(c, stage)
            for i in range(2):
                ring_copy(c, stage, i, place(me), devs[i]).wait_send()
                ring_copy(c, stage, 2 + i, part(me, 0), devs[i]).wait_send()
        for i in range(4):
            core_copy(c, i).wait_send()
    for number in range(4):
        for g in range(GROUPS):
            halo(number, g, 3, OWN, north).wait_send()
            halo(number, g, 5, OWN, north).wait_send()
            for edge, slots in ((last_col, (0, 1, 2)), (first_col, (6, 7, 8))):
                @pl.when(jnp.logical_not(edge))
                def _():
                    for slot in slots:
                        halo(number, g, slot, OWN, north).wait_send()
            if g in RELAYED:
                @pl.when(first_row | last_row)
                def _():
                    row_pass(number, g, 3, north).wait_send()

                @pl.when(first_col | last_col)
                def _():
                    for dr in (-1, 0, 1):
                        col_pass(number, g, dr, OWN, north).wait_send()
    for slot in (0, 1, 2, 3, 5, 6, 7, 8):
        stat(slot, OWN, east).wait_send()


def on_device(q, k, v, out_grad, out_weight, extent, pad):
    shape = q.shape
    flat = lambda a: a.reshape(TOK, a.shape[-1])
    pieces = out_weight.reshape(6, SLABS, SLABW).transpose(1, 0, 2)
    pieces = jnp.pad(pieces, ((0, 0), (0, 10), (0, 0)))
    hbm = pl.BlockSpec(memory_space=pl.ANY)
    smem = pl.BlockSpec(memory_space=pltpu.SMEM)
    vmem = pl.BlockSpec(memory_space=pltpu.VMEM)
    near = pltpu.VMEM((HEADS, 9, TOK, HD), BF)
    dma = pltpu.SemaphoreType.DMA
    out, dq, dk, dv = pl.pallas_call(
        kernel,
        out_shape=(
            jax.ShapeDtypeStruct((TOK, D), BF),
            jax.ShapeDtypeStruct((TOK, E), BF),
            jax.ShapeDtypeStruct((TOK, E), BF),
            jax.ShapeDtypeStruct((TOK, E), BF),
        ),
        in_specs=[smem, smem, hbm, hbm, hbm, hbm, vmem],
        out_specs=(vmem, vmem, vmem, vmem),
        scratch_shapes=[
            near, near, near, near,
            pltpu.VMEM((GROUPS, 2, 4, 4, 96, SLABW), BF),
            pltpu.VMEM((TOK, D), BF),
            pltpu.VMEM((8, 16, SLABW), BF),
            pltpu.VMEM((48, SLABW), BF),
            pltpu.VMEM((GROUPS, TOK, PER * HD), BF),
            pltpu.VMEM((HEADS, TOK, CELLS), BF),
            pltpu.VMEM((TOK, TOK), F32),
            pltpu.VMEM((9, TOK, TOK), F32),
            pltpu.VMEM((16, 128), BF),
            dma((4, HEADS)),
            dma((7,)), dma((7,)), dma((7,)), dma((7,)),
            dma((GROUPS, 2, 4)), dma((GROUPS, 2, 4)),
            dma((GROUPS, 4)), dma((GROUPS, 4)),
            dma((4, GROUPS, 9)), dma((4, GROUPS, 9)),
            dma((9,)), dma((9,)),
            pltpu.VMEM((4, 2, PER, TOK, HD), BF),
            pltpu.VMEM((4, 2, 3, PER, TOK, HD), BF),
            dma((4, 2)), dma((4, 2)), dma((4, 2, 3)), dma((4, 2, 3)),
        ],
        compiler_params=pltpu.CompilerParams(
            collective_id=0, has_side_effects=True, vmem_limit_bytes=60 * 1024 * 1024),
        cost_estimate=pl.CostEstimate(flops=7 * 10**9, bytes_accessed=6 * 10**6, transcendentals=4 * 10**6),
    )(extent, pad, flat(q), flat(k), flat(v), flat(out_grad), pieces)
    return (out.reshape(out_grad.shape), dq.reshape(shape), dk.reshape(shape), dv.reshape(shape))


def solution(mesh):
    cells = P(None, "th", "tw", None)
    return jax.shard_map(
        on_device,
        mesh=mesh,
        in_specs=(cells, cells, cells, cells, P(("th", "tw"), None), P(), P()),
        out_specs=(cells, cells, cells, cells),
        check_vma=False,
    )
```

```python
import functools

import jax
import jax.numpy as jnp
from jax import lax
from jax.experimental import pallas as pl
from jax.experimental.pallas import tpu as pltpu
from jax.sharding import PartitionSpec as P

MESH = pl.DeviceIdType.MESH
HEADS, HD, TOK = 12, 128, 128
GROUPS, PER = 4, 3
D, E = 3072, 1536
SLABS = 8
SLABW = D // SLABS
OWN = 4
RELAYED = (2, 3)
ORDER = (2, 3, 0, 1)
Y_FIRST = (1, 3)
CELLS = 9 * TOK
SIZES = ((9, 7, 4), (9, 9, 6), (12, 12, 12))
MASKED = -1e30
FACTOR = HD ** (-0.5)
BF, F32 = jnp.bfloat16, jnp.float32


def nt(a, b):
    return lax.dot_general(a, b, (((1,), (1,)), ((), ())), preferred_element_type=F32)


def nn(a, b):
    return jnp.dot(a, b, preferred_element_type=F32)


def kernel(
    sizes, ext_ref, pad_ref, q_hbm, k_hbm, v_hbm, g_hbm, w_ref,
    out_ref, dq_ref, dk_ref, dv_ref,
    qn, kn, vn, dn, wb, grads, pieces, block, att, probs, own_stats, stats,
    load_sem, piece_s, piece_r, z_s, z_r, ring_s, ring_r, core_s, core_r, halo_s, halo_r, stat_s, stat_r,
    row_relay, col_relay, natural, place_ref, padded, row_rs, row_rr, col_rs, col_rr,
):
    th, tw = lax.axis_index("th"), lax.axis_index("tw")
    zh, y = th // 4, th % 4
    zl, x, core = tw // 8, (tw // 2) % 4, tw % 2
    z = zh * 2 + zl

    def at(zz, yy, xx, cc):
        return ((zz // 2) * 4 + yy, (zz % 2) * 8 + xx * 2 + cc)

    def tile(dr, dc):
        return ((th + dr + 16) % 16, (tw + dc + 16) % 16)

    north, south, west, east = tile(-1, 0), tile(1, 0), tile(0, -1), tile(0, 1)
    y_up, y_down = (y + 1) % 4, (y + 3) % 4
    x_up, x_down = (x + 1) % 4, (x + 3) % 4
    near_xc = [at(z, y, ((x * 2 + core + i) % 8) // 2, (core + i) % 2) for i in range(1, 8)]
    near_z = [at((z + i) % 8, y, x, core) for i in range(1, 8)]
    near_y = [at(z, y_up, x, core), at(z, y_down, x, core)]

    def remote(src, dst, send, recv, device):
        return pltpu.make_async_remote_copy(
            src_ref=src, dst_ref=dst, send_sem=send, recv_sem=recv,
            device_id=device, device_id_type=MESH,
        )

    barrier = pltpu.get_barrier_semaphore()
    greeted = [north, south, west, east] + near_xc + near_z + near_y
    for target in greeted:
        pl.semaphore_signal(barrier, inc=1, device_id=target, device_id_type=MESH)
    loads = []
    for number, hbm in enumerate((k_hbm, v_hbm, q_hbm)):
        for h in range(HEADS):
            loads.append(pltpu.make_async_copy(
                hbm.at[:, pl.ds(h * HD, HD)], natural.at[number, h], load_sem.at[number, h]))
    loads.append(pltpu.make_async_copy(g_hbm, grads, load_sem.at[3, 0]))
    mine = x * 2 + core
    slab = core * 4 + x
    for copy in loads:
        copy.start()
    padded[...] = jnp.zeros_like(padded)
    padded[:, 0:6, :] = w_ref[...]
    own_piece = pltpu.make_async_copy(padded.at[slab], pieces.at[mine], load_sem.at[3, 1])
    own_piece.start()

    n_rows, n_cols, n_both = sizes
    row_only, col_only = n_rows - n_both, n_cols - n_both
    none_left = HEADS - n_rows - col_only
    in_rows = [ext_ref[0, h] for h in range(HEADS)]
    in_cols = [ext_ref[1, h] for h in range(HEADS)]
    used = [jnp.int32(0)] * 4
    places = [jnp.int32(0)] * HEADS
    starts = (0, row_only, n_rows, n_rows + col_only)
    room = (row_only, n_both, col_only, none_left)
    for wanted_rows, wanted_cols, pools in ((1, 1, (1,)), (1, 0, (0, 1)), (0, 1, (2, 1)), (0, 0, (3, 0, 2, 1))):
        for h in range(HEADS):
            open_now = (in_rows[h] == wanted_rows) & (in_cols[h] == wanted_cols)
            for pool in pools:
                take = open_now if pool == pools[-1] else open_now & (used[pool] < room[pool])
                places[h] = jnp.where(take, starts[pool] + used[pool], places[h])
                used[pool] = used[pool] + take.astype(jnp.int32)
                open_now = open_now & jnp.logical_not(take)
    for h in range(HEADS):
        place_ref[h] = places[h]
    heads_at = [
        sum(jnp.where(places[h] == p, h, 0) for h in range(HEADS)) for p in range(HEADS)]

    ranges = {}
    for j in (3, 5):
        ranges[j] = (0, n_rows)
    for j in (1, 7):
        ranges[j] = (row_only, n_rows + col_only)
    for j in (0, 2, 6, 8):
        ranges[j] = (row_only, n_rows)
    for near in (kn, vn, qn):
        for j, (low, high) in ranges.items():
            if low:
                near[0:low, j] = jnp.zeros((low, TOK, HD), BF)
            if high < HEADS:
                near[high:HEADS, j] = jnp.zeros((HEADS - high, TOK, HD), BF)
    for edge, slots in ((tw == 0, (0, 1, 2)), (tw == 15, (6, 7, 8))):
        @pl.when(edge)
        def _():
            for near in (kn, vn, qn, dn):
                for j in slots:
                    near[:, j] = jnp.zeros((HEADS, TOK, HD), BF)
    for copy in loads:
        copy.wait()
    own_piece.wait()
    for p in range(HEADS):
        for number, near in enumerate((kn, vn, qn)):
            near[p, OWN] = natural[number, heads_at[p]]
    pl.semaphore_wait(barrier, len(greeted))

    nears = (kn, vn, qn, dn)

    def span(number, g, slot):
        if number == 3:
            return g * PER, PER
        low, high = ranges[slot]
        first = low + (high - low) * g // GROUPS
        return first, low + (high - low) * (g + 1) // GROUPS - first

    def halo(number, g, slot, source, device):
        near = nears[number]
        heads = pl.ds(*span(number, g, slot))
        return remote(near.at[heads, source], near.at[heads, slot],
                      halo_s.at[number, g, slot], halo_r.at[number, g, slot], device)

    first_row, last_row = y == 0, y == 3
    first_col, last_col = tw == 0, tw == 15
    cross_east, cross_west = tw == 7, tw == 8

    def via(number, g, slot, source, space, send, recv, device):
        first, count = span(number, g, slot)
        return remote(nears[number].at[pl.ds(first, count), source], space.at[pl.ds(0, count)], send, recv, device)

    def rows(number, g):
        if g in RELAYED:
            i = g - RELAYED[0]
            for slot, crossing, straight, device in (
                (3, last_row, south, tile(-3, 0)), (5, first_row, north, tile(3, 0))):
                @pl.when(crossing)
                def _():
                    via(number, g, slot, OWN, row_relay.at[number, i], halo_s.at[number, g, slot],
                        row_rr.at[number, i], device).start()

                @pl.when(jnp.logical_not(crossing))
                def _():
                    halo(number, g, slot, OWN, straight).start()
        else:
            halo(number, g, 3, OWN, south).start()
            halo(number, g, 5, OWN, north).start()

    def row_pass(number, g, slot, device):
        i = g - RELAYED[0]
        first, count = span(number, g, slot)
        return remote(row_relay.at[number, i, pl.ds(0, count)], nears[number].at[pl.ds(first, count), slot],
                      row_rs.at[number, i], halo_r.at[number, g, slot], device)

    def pass_rows(number, g):
        if g not in RELAYED:
            return
        i = g - RELAYED[0]
        for slot, crossing, device in ((3, first_row, tile(4, 0)), (5, last_row, tile(-4, 0))):
            @pl.when(crossing)
            def _():
                via(number, g, slot, OWN, row_relay.at[number, i], row_rs.at[number, i],
                    row_rr.at[number, i], north).wait_recv()
                row_pass(number, g, slot, device).start()

    def columns(number, g, dr):
        for slot, crossing, edge, straight, device in (
            (1 + dr, cross_east, last_col, east, tile(0, -7)),
            (7 + dr, cross_west, first_col, west, tile(0, 7))):
            if g in RELAYED:
                i = g - RELAYED[0]

                @pl.when(crossing)
                def _():
                    via(number, g, slot, OWN + dr, col_relay.at[number, i, dr + 1],
                        halo_s.at[number, g, slot], col_rr.at[number, i, dr + 1], device).start()

                @pl.when(jnp.logical_not(crossing | edge))
                def _():
                    halo(number, g, slot, OWN + dr, straight).start()
            else:
                @pl.when(jnp.logical_not(edge))
                def _():
                    halo(number, g, slot, OWN + dr, straight).start()

    def col_pass(number, g, dr, slot, device):
        i = g - RELAYED[0]
        first, count = span(number, g, slot)
        return remote(col_relay.at[number, i, dr + 1, pl.ds(0, count)], nears[number].at[pl.ds(first, count), slot],
                      col_rs.at[number, i, dr + 1], halo_r.at[number, g, slot], device)

    def pass_columns(number, g, drs=(0, -1, 1)):
        if g not in RELAYED:
            return
        i = g - RELAYED[0]
        for base, edge, device in ((1, first_col, tile(0, 8)), (7, last_col, tile(0, -8))):
            @pl.when(edge)
            def _():
                for dr in drs:
                    via(number, g, base + dr, OWN, col_relay.at[number, i, dr + 1], col_rs.at[number, i, dr + 1],
                        col_rr.at[number, i, dr + 1], north).wait_recv()
                    col_pass(number, g, dr, base + dr, device).start()

    def arrived(number, g, slot):
        halo(number, g, slot, OWN, north).wait_recv()

    def rows_then_columns(number, g):
        arrived(number, g, 3)
        columns(number, g, -1)
        arrived(number, g, 5)
        columns(number, g, 1)

    def all_rows_then_columns(number):
        for g in range(GROUPS):
            arrived(number, g, 3)
            arrived(number, g, 5)
        for g in ORDER:
            columns(number, g, -1)
            columns(number, g, 1)

    def all_columns(number, g):
        @pl.when(jnp.logical_not(first_col))
        def _():
            for slot in (0, 1, 2):
                arrived(number, g, slot)

        @pl.when(jnp.logical_not(last_col))
        def _():
            for slot in (6, 7, 8):
                arrived(number, g, slot)

    for i in range(1, 8):
        t = (mine + i) % 8
        remote(padded.at[(t % 2) * 4 + t // 2], pieces.at[mine], piece_s.at[i - 1], piece_r.at[i - 1],
               near_xc[i - 1]).start()
    for number in (0, 1):
        for g in ORDER:
            rows(number, g)
            columns(number, g, 0)
    for i in range(1, 8):
        remote(padded.at[0], pieces.at[(mine + 8 - i) % 8], piece_s.at[i - 1], piece_r.at[i - 1],
               near_xc[i - 1]).wait_recv()
    block[...] = jnp.concatenate(
        [pieces[t].astype(F32)[0:6] for t in range(8)], axis=0).astype(BF)

    def z_place(zz):
        return wb.at[zz // 2, core, x, y, pl.ds((zz % 2) * 48, 48)]

    own_place = pltpu.make_async_copy(block, z_place(z), load_sem.at[3, 2])
    own_place.start()
    for i in range(1, 8):
        remote(block, z_place(z), z_s.at[i - 1], z_r.at[i - 1], near_z[i - 1]).start()
    own_place.wait()
    for number in (0, 1):
        for g in RELAYED:
            pass_rows(number, g)
            pass_columns(number, g, (0,))
    for i in range(1, 8):
        remote(block, z_place((z + 8 - i) % 8), z_s.at[i - 1], z_r.at[i - 1], near_z[i - 1]).wait_recv()

    y_dev = (at(z, y_up, x, core), at(z, y_down, x, core))
    x_dev = (at(z, y, x_up, core), at(z, y, x_down, core))
    other = at(z, y, x, 1 - core)
    half = lambda i: pl.ds(i * 2, 2)

    def ring(c, stage):
        along_y = (c in Y_FIRST) == (stage == 0)
        if along_y:
            me, devs = y, y_dev
            if stage == 0:
                place = lambda p: wb.at[c, core, x, p]
                part = lambda p, i: wb.at[c, core, x, p, pl.ds(i * 48, 48)]
            else:
                place = lambda p: wb.at[c, core, :, p]
                part = lambda p, i: wb.at[c, core, half(i), p]
        else:
            me, devs = x, x_dev
            if stage == 0:
                place = lambda p: wb.at[c, core, p, y]
                part = lambda p, i: wb.at[c, core, p, y, pl.ds(i * 48, 48)]
            else:
                place = lambda p: wb.at[c, core, p]
                part = lambda p, i: wb.at[c, core, p, half(i)]
        return place, part, me, devs

    def ring_copy(c, stage, i, ref, device):
        return remote(ref, ref, ring_s.at[c, stage, i], ring_r.at[c, stage, i], device)

    def ring_start(c, stage):
        place, part, me, devs = ring(c, stage)
        ring_copy(c, stage, 0, place(me), devs[0]).start()
        ring_copy(c, stage, 1, place(me), devs[1]).start()

    def ring_relay(c, stage):
        place, part, me, devs = ring(c, stage)
        down, up = (me + 3) % 4, (me + 1) % 4
        ring_copy(c, stage, 0, place(down), devs[0]).wait_recv()
        ring_copy(c, stage, 2, part(down, 0), devs[0]).start()
        ring_copy(c, stage, 1, place(up), devs[1]).wait_recv()
        ring_copy(c, stage, 3, part(up, 1), devs[1]).start()
        return place(down), place(up)

    def ring_end(c, stage):
        place, part, me, devs = ring(c, stage)
        far = (me + 2) % 4
        ring_copy(c, stage, 2, part(far, 0), devs[0]).wait_recv()
        ring_copy(c, stage, 3, part(far, 1), devs[1]).wait_recv()
        return place(far)

    def core_copy(c, i):
        place, part, me, devs = ring(c, 1)
        ref = place((me + i) % 4)
        return remote(ref, ref, core_s.at[c, i], core_r.at[c, i], other)

    def core_arrival(c, i):
        along_y = c not in Y_FIRST
        p = ((y if along_y else x) + i) % 4
        ref = wb.at[c, 1 - core, :, p] if along_y else wb.at[c, 1 - core, p]
        return remote(ref, ref, core_s.at[c, i], core_r.at[c, i], other)

    for c in range(GROUPS):
        ring_start(c, 0)
    for g in ORDER:
        rows(2, g)
        columns(2, g, 0)
    for c in range(GROUPS):
        ring_relay(c, 0)
    for c in range(GROUPS):
        ring_end(c, 0)
        ring_start(c, 1)
        core_copy(c, 0).start()
    for g in RELAYED:
        pass_rows(2, g)
        pass_columns(2, g, (0,))
    for c in range(GROUPS):
        if c in (0, 2):
            all_rows_then_columns(c // 2)
        ring_relay(c, 1)
        core_copy(c, 1).start()
        core_copy(c, 3).start()
    for c in range(GROUPS):
        ring_end(c, 1)
        core_copy(c, 2).start()
        for i in range(4):
            core_arrival(c, i).wait_recv()
        total = jnp.zeros((TOK, PER * HD), F32)
        for s in range(SLABS):
            w = wb[c, s // 4, s % 4].reshape(PER * HD, SLABW)
            total += nt(grads[:, s * SLABW:(s + 1) * SLABW], w)
        for i in range(PER):
            dn[c * PER + i, OWN] = total[:, i * HD:(i + 1) * HD].astype(BF)
        rows(3, c)
        columns(3, c, 0)
        pass_columns(0, c, (-1, 1))
        pass_columns(1, c, (-1, 1))
        if c == 1:
            all_rows_then_columns(2)

    lane = lax.broadcasted_iota(jnp.int32, (1, CELLS), 1)
    slot, token = lane // TOK, lane % TOK
    dr, dc = slot % 3 - 1, slot // 3 - 1
    row = (th + dr) * 8 + (token // 8) % 8
    col = (tw + dc) * 8 + token % 8
    limit_rows, limit_cols = 128 - pad_ref[0], 128 - pad_ref[1]
    key_ok = (row >= 0) & (row < limit_rows) & (col >= 0) & (col < limit_cols)
    query_ok = (row >= 0) & (row < 128) & (col >= 0) & (col < 128)
    key_bias = jnp.where(key_ok, 0.0, MASKED)
    query_bias = jnp.where(query_ok, 0.0, MASKED)
    far_rows, far_cols = jnp.abs(dr), jnp.abs(dc)

    def window(h, bias):
        inside = (far_rows <= ext_ref[0, h]) & (far_cols <= ext_ref[1, h])
        return jnp.where(inside, bias, MASKED)

    lane_of = lax.broadcasted_iota(jnp.int32, (TOK, TOK), 1)

    def forward(g, found):
        for i in range(PER):
            h = g * PER + i
            p = place_ref[h]
            s = nt(natural[2, h], kn[p].reshape(CELLS, HD)) * FACTOR + window(h, key_bias)
            top = jnp.max(s, axis=1, keepdims=True)
            e = jnp.exp(s - top)
            summed = jnp.sum(e, axis=1, keepdims=True)
            w = (e * (1.0 / summed)).astype(BF)
            probs[h] = w
            o = nn(w, vn[p].reshape(CELLS, HD)).astype(BF)
            att[g, :, i * HD:(i + 1) * HD] = o
            correction = jnp.sum(o.astype(F32) * dn[h, OWN].astype(F32), axis=1, keepdims=True)
            found = jnp.where(lane_of == h, top + jnp.log(summed), found)
            found = jnp.where(lane_of == HEADS + h, correction, found)
        return found

    for g in RELAYED:
        pass_rows(3, g)
        pass_columns(3, g, (0,))
    for g in range(GROUPS):
        all_columns(0, g)
        all_columns(1, g)
    found = forward(0, jnp.zeros((TOK, TOK), F32))
    for g in RELAYED:
        pass_columns(2, g, (-1, 1))
    rows_then_columns(3, 0)
    rows_then_columns(3, 1)
    found = forward(1, found)
    rows_then_columns(3, 2)
    rows_then_columns(3, 3)
    found = forward(2, found)
    found = forward(3, found)
    own_stats[...] = found
    stats[OWN] = found.T

    def stat(slot, source, device):
        return remote(stats.at[source], stats.at[slot], stat_s.at[slot], stat_r.at[slot], device)

    stat(3, OWN, south).start()
    stat(5, OWN, north).start()
    stat(1, OWN, east).start()
    stat(7, OWN, west).start()

    for g in RELAYED:
        pass_columns(3, g, (-1, 1))

    for s in range(SLABS):
        total = jnp.zeros((TOK, SLABW), F32)
        for c in range(GROUPS):
            total += nn(att[c], wb[c, s // 4, s % 4].reshape(PER * HD, SLABW))
        out_ref[:, s * SLABW:(s + 1) * SLABW] = total.astype(BF)

    stat(3, OWN, south).wait_recv()
    stat(0, 3, east).start()
    stat(6, 3, west).start()
    stat(5, OWN, north).wait_recv()
    stat(2, 5, east).start()
    stat(8, 5, west).start()

    def query_part(g, carry):
        for i in range(PER):
            h = g * PER + i
            correction = jnp.sum(jnp.where(lane_of == HEADS + h, own_stats[...], 0.0), axis=1, keepdims=True)
            p = place_ref[h]
            dp = nt(dn[h, OWN], vn[p].reshape(CELLS, HD))
            ds = (probs[h].astype(F32) * (dp - correction)).astype(BF)
            dq = nn(ds, kn[p].reshape(CELLS, HD)) * FACTOR
            dq_ref[:, pl.ds(pl.multiple_of(h * HD, HD), HD)] = dq.astype(BF)
        return carry

    lax.fori_loop(0, GROUPS, query_part, 0)

    for slot in (0, 1, 2, 6, 7, 8):
        stat(slot, OWN, east).wait_recv()
    cell = lax.broadcasted_iota(jnp.int32, (TOK, 1), 0)
    own_ok = (th * 8 + (cell // 8) % 8 < limit_rows) & (tw * 8 + cell % 8 < limit_cols)

    for g in range(GROUPS):
        all_columns(2, g)

    def key_part(g, carry):
        all_columns(3, g)
        for i in range(PER):
            h = g * PER + i
            totals = jnp.concatenate([stats[j, pl.ds(h, 1)] for j in range(9)], axis=1)
            corrections = jnp.concatenate([stats[j, pl.ds(HEADS + h, 1)] for j in range(9)], axis=1)
            shift = window(h, query_bias) - totals
            qs = qn[place_ref[h]].reshape(CELLS, HD)
            ds_near = dn[h].reshape(CELLS, HD)
            w = jnp.exp(nt(natural[0, h], qs) * FACTOR + shift)
            dp = nt(natural[1, h], ds_near)
            ds = (w * (dp - corrections)).astype(BF)
            dk = jnp.where(own_ok, nn(ds, qs) * FACTOR, 0.0)
            dv = jnp.where(own_ok, nn(w.astype(BF), ds_near), 0.0)
            at_h = pl.ds(pl.multiple_of(h * HD, HD), HD)
            dk_ref[:, at_h] = dk.astype(BF)
            dv_ref[:, at_h] = dv.astype(BF)
        return carry

    lax.fori_loop(0, GROUPS, key_part, 0)

    for i in range(1, 8):
        remote(padded.at[0], pieces.at[0], piece_s.at[i - 1], piece_r.at[i - 1], near_xc[i - 1]).wait_send()
        remote(block, z_place(z), z_s.at[i - 1], z_r.at[i - 1], near_z[i - 1]).wait_send()
    for c in range(GROUPS):
        for stage in range(2):
            place, part, me, devs = ring(c, stage)
            for i in range(2):
                ring_copy(c, stage, i, place(me), devs[i]).wait_send()
                ring_copy(c, stage, 2 + i, part(me, 0), devs[i]).wait_send()
        for i in range(4):
            core_copy(c, i).wait_send()
    for number in range(4):
        for g in range(GROUPS):
            halo(number, g, 3, OWN, north).wait_send()
            halo(number, g, 5, OWN, north).wait_send()
            for edge, slots in ((last_col, (0, 1, 2)), (first_col, (6, 7, 8))):
                @pl.when(jnp.logical_not(edge))
                def _():
                    for slot in slots:
                        halo(number, g, slot, OWN, north).wait_send()
            if g in RELAYED:
                @pl.when(first_row | last_row)
                def _():
                    row_pass(number, g, 3, north).wait_send()

                @pl.when(first_col | last_col)
                def _():
                    for dr in (-1, 0, 1):
                        col_pass(number, g, dr, 1 + dr, north).wait_send()
    for slot in (0, 1, 2, 3, 5, 6, 7, 8):
        stat(slot, OWN, east).wait_send()


def run(number, q, k, v, out_grad, pieces, extent, pad):
    hbm = pl.BlockSpec(memory_space=pl.ANY)
    smem = pl.BlockSpec(memory_space=pltpu.SMEM)
    vmem = pl.BlockSpec(memory_space=pltpu.VMEM)
    near = pltpu.VMEM((HEADS, 9, TOK, HD), BF)
    dma = pltpu.SemaphoreType.DMA
    return pl.pallas_call(
        functools.partial(kernel, SIZES[number]),
        out_shape=(
            jax.ShapeDtypeStruct((TOK, D), BF),
            jax.ShapeDtypeStruct((TOK, E), BF),
            jax.ShapeDtypeStruct((TOK, E), BF),
            jax.ShapeDtypeStruct((TOK, E), BF),
        ),
        in_specs=[smem, smem, hbm, hbm, hbm, hbm, vmem],
        out_specs=(vmem, vmem, vmem, vmem),
        scratch_shapes=[
            near, near, near, near,
            pltpu.VMEM((GROUPS, 2, 4, 4, 96, SLABW), BF),
            pltpu.VMEM((TOK, D), BF),
            pltpu.VMEM((8, 16, SLABW), BF),
            pltpu.VMEM((48, SLABW), BF),
            pltpu.VMEM((GROUPS, TOK, PER * HD), BF),
            pltpu.VMEM((HEADS, TOK, CELLS), BF),
            pltpu.VMEM((TOK, TOK), F32),
            pltpu.VMEM((9, TOK, TOK), F32),
            dma((4, HEADS)),
            dma((7,)), dma((7,)), dma((7,)), dma((7,)),
            dma((GROUPS, 2, 4)), dma((GROUPS, 2, 4)),
            dma((GROUPS, 4)), dma((GROUPS, 4)),
            dma((4, GROUPS, 9)), dma((4, GROUPS, 9)),
            dma((9,)), dma((9,)),
            pltpu.VMEM((4, 2, PER, TOK, HD), BF),
            pltpu.VMEM((4, 2, 3, PER, TOK, HD), BF),
            pltpu.VMEM((3, HEADS, TOK, HD), BF),
            pltpu.SMEM((HEADS,), jnp.int32),
            pltpu.VMEM((8, 16, SLABW), BF),
            dma((4, 2)), dma((4, 2)), dma((4, 2, 3)), dma((4, 2, 3)),
        ],
        compiler_params=pltpu.CompilerParams(
            collective_id=number, has_side_effects=True, vmem_limit_bytes=60 * 1024 * 1024),
        cost_estimate=pl.CostEstimate(flops=7 * 10**9, bytes_accessed=6 * 10**6, transcendentals=4 * 10**6),
    )(extent, pad, q, k, v, out_grad, pieces)


def choice(extent):
    in_rows, in_cols = extent[0], extent[1]
    both = jnp.sum(in_rows * in_cols)
    rows_only, cols_only = jnp.sum(in_rows) - both, jnp.sum(in_cols) - both
    number = jnp.int32(len(SIZES) - 1)
    for i in reversed(range(len(SIZES) - 1)):
        n_rows, n_cols, n_both = SIZES[i]
        beyond = jnp.maximum(rows_only - (n_rows - n_both), 0) + jnp.maximum(cols_only - (n_cols - n_both), 0)
        number = jnp.where(beyond + both <= n_both, i, number)
    return number


def on_device(q, k, v, out_grad, out_weight, extent, pad):
    shape = q.shape
    flat = lambda a: a.reshape(TOK, a.shape[-1])
    pieces = out_weight.reshape(6, SLABS, SLABW).transpose(1, 0, 2)
    out, dq, dk, dv = lax.switch(
        choice(extent), [functools.partial(run, i) for i in range(len(SIZES))],
        flat(q), flat(k), flat(v), flat(out_grad), pieces, extent, pad)
    return (out.reshape(out_grad.shape), dq.reshape(shape), dk.reshape(shape), dv.reshape(shape))


def solution(mesh):
    cells = P(None, "th", "tw", None)
    return jax.shard_map(
        on_device,
        mesh=mesh,
        in_specs=(cells, cells, cells, cells, P(("th", "tw"), None), P(), P()),
        out_specs=(cells, cells, cells, cells),
        check_vma=False,
    )
```

```python
import functools

import jax
import jax.numpy as jnp
from jax import lax
from jax.experimental import pallas as pl
from jax.experimental.pallas import tpu as pltpu
from jax.sharding import PartitionSpec as P

MESH = pl.DeviceIdType.MESH
HEADS, HD, TOK = 12, 128, 128
GROUPS, PER = 4, 3
D, E = 3072, 1536
SLABS = 8
SLABW = D // SLABS
OWN = 4
RELAYED = (2, 3)
ORDER = (2, 3, 0, 1)
Y_FIRST = (1, 3)
CELLS = 9 * TOK
SIZES = ((9, 7, 4), (9, 9, 6), (12, 12, 12))
MASKED = -1e30
FACTOR = HD ** (-0.5)
BF, F32 = jnp.bfloat16, jnp.float32


def nt(a, b):
    return lax.dot_general(a, b, (((1,), (1,)), ((), ())), preferred_element_type=F32)


def nn(a, b):
    return jnp.dot(a, b, preferred_element_type=F32)


def kernel(
    sizes, ext_ref, pad_ref, q_hbm, k_hbm, v_hbm, g_hbm, w_ref,
    out_ref, dq_ref, dk_ref, dv_ref,
    qn, kn, vn, dn, wb, grads, pieces, block, att, probs, own_stats, stats,
    load_sem, piece_s, piece_r, z_s, z_r, ring_s, ring_r, core_s, core_r, halo_s, halo_r, stat_s, stat_r,
    row_relay, col_relay, natural, place_ref, padded, row_rs, row_rr, col_rs, col_rr,
):
    th, tw = lax.axis_index("th"), lax.axis_index("tw")
    zh, y = th // 4, th % 4
    zl, x, core = tw // 8, (tw // 2) % 4, tw % 2
    z = zh * 2 + zl

    def at(zz, yy, xx, cc):
        return ((zz // 2) * 4 + yy, (zz % 2) * 8 + xx * 2 + cc)

    def tile(dr, dc):
        return ((th + dr + 16) % 16, (tw + dc + 16) % 16)

    north, south, west, east = tile(-1, 0), tile(1, 0), tile(0, -1), tile(0, 1)
    y_up, y_down = (y + 1) % 4, (y + 3) % 4
    x_up, x_down = (x + 1) % 4, (x + 3) % 4
    near_xc = [at(z, y, ((x * 2 + core + i) % 8) // 2, (core + i) % 2) for i in range(1, 8)]
    near_z = [at((z + i) % 8, y, x, core) for i in range(1, 8)]
    near_y = [at(z, y_up, x, core), at(z, y_down, x, core)]

    def remote(src, dst, send, recv, device):
        return pltpu.make_async_remote_copy(
            src_ref=src, dst_ref=dst, send_sem=send, recv_sem=recv,
            device_id=device, device_id_type=MESH,
        )

    barrier = pltpu.get_barrier_semaphore()
    corners = [tile(-1, -1), tile(-1, 1), tile(1, -1), tile(1, 1)]
    greeted = [north, south, west, east] + near_xc + near_z + near_y + corners
    for target in greeted:
        pl.semaphore_signal(barrier, inc=1, device_id=target, device_id_type=MESH)
    loads = []
    for number, hbm in enumerate((k_hbm, v_hbm, q_hbm)):
        for h in range(HEADS):
            loads.append(pltpu.make_async_copy(
                hbm.at[:, pl.ds(h * HD, HD)], natural.at[number, h], load_sem.at[number, h]))
    loads.append(pltpu.make_async_copy(g_hbm, grads, load_sem.at[3, 0]))
    mine = x * 2 + core
    slab = core * 4 + x
    for copy in loads:
        copy.start()
    padded[...] = jnp.zeros_like(padded)
    padded[:, 0:6, :] = w_ref[...]
    own_piece = pltpu.make_async_copy(padded.at[slab], pieces.at[mine], load_sem.at[3, 1])
    own_piece.start()

    n_rows, n_cols, n_both = sizes
    row_only, col_only = n_rows - n_both, n_cols - n_both
    none_left = HEADS - n_rows - col_only
    in_rows = [ext_ref[0, h] for h in range(HEADS)]
    in_cols = [ext_ref[1, h] for h in range(HEADS)]
    used = [jnp.int32(0)] * 4
    places = [jnp.int32(0)] * HEADS
    starts = (0, row_only, n_rows, n_rows + col_only)
    room = (row_only, n_both, col_only, none_left)
    for wanted_rows, wanted_cols, pools in ((1, 1, (1,)), (1, 0, (0, 1)), (0, 1, (2, 1)), (0, 0, (3, 0, 2, 1))):
        for h in range(HEADS):
            open_now = (in_rows[h] == wanted_rows) & (in_cols[h] == wanted_cols)
            for pool in pools:
                take = open_now if pool == pools[-1] else open_now & (used[pool] < room[pool])
                places[h] = jnp.where(take, starts[pool] + used[pool], places[h])
                used[pool] = used[pool] + take.astype(jnp.int32)
                open_now = open_now & jnp.logical_not(take)
    for h in range(HEADS):
        place_ref[h] = places[h]
    heads_at = [
        sum(jnp.where(places[h] == p, h, 0) for h in range(HEADS)) for p in range(HEADS)]

    ranges = {}
    for j in (3, 5):
        ranges[j] = (0, n_rows)
    for j in (1, 7):
        ranges[j] = (row_only, n_rows + col_only)
    for j in (0, 2, 6, 8):
        ranges[j] = (row_only, n_rows)
    for near in (kn, vn, qn):
        for j, (low, high) in ranges.items():
            if low:
                near[0:low, j] = jnp.zeros((low, TOK, HD), BF)
            if high < HEADS:
                near[high:HEADS, j] = jnp.zeros((HEADS - high, TOK, HD), BF)
    for edge, slots in ((tw == 0, (0, 1, 2)), (tw == 15, (6, 7, 8))):
        @pl.when(edge)
        def _():
            for near in (kn, vn, qn, dn):
                for j in slots:
                    near[:, j] = jnp.zeros((HEADS, TOK, HD), BF)
    for copy in loads:
        copy.wait()
    own_piece.wait()
    for p in range(HEADS):
        for number, near in enumerate((kn, vn, qn)):
            near[p, OWN] = natural[number, heads_at[p]]
    pl.semaphore_wait(barrier, len(greeted))

    nears = (kn, vn, qn, dn)

    def span(number, g, slot):
        if number == 3:
            return g * PER, PER
        low, high = ranges[slot]
        first = low + (high - low) * g // GROUPS
        return first, low + (high - low) * (g + 1) // GROUPS - first

    def halo(number, g, slot, source, device):
        near = nears[number]
        heads = pl.ds(*span(number, g, slot))
        return remote(near.at[heads, source], near.at[heads, slot],
                      halo_s.at[number, g, slot], halo_r.at[number, g, slot], device)

    first_row, last_row = y == 0, y == 3
    first_col, last_col = tw == 0, tw == 15
    cross_east, cross_west = tw == 7, tw == 8

    def via(number, g, slot, source, space, send, recv, device):
        first, count = span(number, g, slot)
        return remote(nears[number].at[pl.ds(first, count), source], space.at[pl.ds(0, count)], send, recv, device)

    def rows(number, g):
        if g in RELAYED:
            i = g - RELAYED[0]
            for slot, crossing, straight, device in (
                (3, last_row, south, tile(-3, 0)), (5, first_row, north, tile(3, 0))):
                @pl.when(crossing)
                def _():
                    via(number, g, slot, OWN, row_relay.at[number, i], halo_s.at[number, g, slot],
                        row_rr.at[number, i], device).start()

                @pl.when(jnp.logical_not(crossing))
                def _():
                    halo(number, g, slot, OWN, straight).start()
        else:
            halo(number, g, 3, OWN, south).start()
            halo(number, g, 5, OWN, north).start()

    def row_pass(number, g, slot, device):
        i = g - RELAYED[0]
        first, count = span(number, g, slot)
        return remote(row_relay.at[number, i, pl.ds(0, count)], nears[number].at[pl.ds(first, count), slot],
                      row_rs.at[number, i], halo_r.at[number, g, slot], device)

    def pass_rows(number, g):
        if g not in RELAYED:
            return
        i = g - RELAYED[0]
        for slot, crossing, device in ((3, first_row, tile(4, 0)), (5, last_row, tile(-4, 0))):
            @pl.when(crossing)
            def _():
                via(number, g, slot, OWN, row_relay.at[number, i], row_rs.at[number, i],
                    row_rr.at[number, i], north).wait_recv()
                row_pass(number, g, slot, device).start()

    def columns(number, g, dr):
        for slot, crossing, edge, straight, device in (
            (1 + dr, cross_east, last_col, east, tile(0, -7)),
            (7 + dr, cross_west, first_col, west, tile(0, 7))):
            if g in RELAYED:
                i = g - RELAYED[0]

                @pl.when(crossing)
                def _():
                    via(number, g, slot, OWN + dr, col_relay.at[number, i, dr + 1],
                        halo_s.at[number, g, slot], col_rr.at[number, i, dr + 1], device).start()

                @pl.when(jnp.logical_not(crossing | edge))
                def _():
                    halo(number, g, slot, OWN + dr, straight).start()
            else:
                @pl.when(jnp.logical_not(edge))
                def _():
                    halo(number, g, slot, OWN + dr, straight).start()

    def col_pass(number, g, dr, slot, device):
        i = g - RELAYED[0]
        first, count = span(number, g, slot)
        return remote(col_relay.at[number, i, dr + 1, pl.ds(0, count)], nears[number].at[pl.ds(first, count), slot],
                      col_rs.at[number, i, dr + 1], halo_r.at[number, g, slot], device)

    def pass_columns(number, g, drs=(0, -1, 1)):
        if g not in RELAYED:
            return
        i = g - RELAYED[0]
        for base, edge, device in ((1, first_col, tile(0, 8)), (7, last_col, tile(0, -8))):
            @pl.when(edge)
            def _():
                for dr in drs:
                    via(number, g, base + dr, OWN, col_relay.at[number, i, dr + 1], col_rs.at[number, i, dr + 1],
                        col_rr.at[number, i, dr + 1], north).wait_recv()
                    col_pass(number, g, dr, base + dr, device).start()

    def arrived(number, g, slot):
        halo(number, g, slot, OWN, north).wait_recv()

    def rows_then_columns(number, g):
        arrived(number, g, 3)
        columns(number, g, -1)
        arrived(number, g, 5)
        columns(number, g, 1)

    def all_rows_then_columns(number):
        for g in range(GROUPS):
            arrived(number, g, 3)
            arrived(number, g, 5)
        for g in ORDER:
            columns(number, g, -1)
            columns(number, g, 1)

    def all_columns(number, g):
        @pl.when(jnp.logical_not(first_col))
        def _():
            for slot in (0, 1, 2):
                arrived(number, g, slot)

        @pl.when(jnp.logical_not(last_col))
        def _():
            for slot in (6, 7, 8):
                arrived(number, g, slot)

    for i in range(1, 8):
        t = (mine + i) % 8
        remote(padded.at[(t % 2) * 4 + t // 2], pieces.at[mine], piece_s.at[i - 1], piece_r.at[i - 1],
               near_xc[i - 1]).start()
    for number in (0, 1):
        for g in ORDER:
            rows(number, g)
            columns(number, g, 0)
    for i in range(1, 8):
        remote(padded.at[0], pieces.at[(mine + 8 - i) % 8], piece_s.at[i - 1], piece_r.at[i - 1],
               near_xc[i - 1]).wait_recv()
    block[...] = jnp.concatenate(
        [pieces[t].astype(F32)[0:6] for t in range(8)], axis=0).astype(BF)

    def z_place(zz):
        return wb.at[zz // 2, core, x, y, pl.ds((zz % 2) * 48, 48)]

    own_place = pltpu.make_async_copy(block, z_place(z), load_sem.at[3, 2])
    own_place.start()
    for i in range(1, 8):
        remote(block, z_place(z), z_s.at[i - 1], z_r.at[i - 1], near_z[i - 1]).start()
    own_place.wait()
    for number in (0, 1):
        for g in RELAYED:
            pass_rows(number, g)
            pass_columns(number, g, (0,))
    for i in range(1, 8):
        remote(block, z_place((z + 8 - i) % 8), z_s.at[i - 1], z_r.at[i - 1], near_z[i - 1]).wait_recv()

    y_dev = (at(z, y_up, x, core), at(z, y_down, x, core))
    x_dev = (at(z, y, x_up, core), at(z, y, x_down, core))
    other = at(z, y, x, 1 - core)
    half = lambda i: pl.ds(i * 2, 2)

    def ring(c, stage):
        along_y = (c in Y_FIRST) == (stage == 0)
        if along_y:
            me, devs = y, y_dev
            if stage == 0:
                place = lambda p: wb.at[c, core, x, p]
                part = lambda p, i: wb.at[c, core, x, p, pl.ds(i * 48, 48)]
            else:
                place = lambda p: wb.at[c, core, :, p]
                part = lambda p, i: wb.at[c, core, half(i), p]
        else:
            me, devs = x, x_dev
            if stage == 0:
                place = lambda p: wb.at[c, core, p, y]
                part = lambda p, i: wb.at[c, core, p, y, pl.ds(i * 48, 48)]
            else:
                place = lambda p: wb.at[c, core, p]
                part = lambda p, i: wb.at[c, core, p, half(i)]
        return place, part, me, devs

    def ring_copy(c, stage, i, ref, device):
        return remote(ref, ref, ring_s.at[c, stage, i], ring_r.at[c, stage, i], device)

    def ring_start(c, stage):
        place, part, me, devs = ring(c, stage)
        ring_copy(c, stage, 0, place(me), devs[0]).start()
        ring_copy(c, stage, 1, place(me), devs[1]).start()

    def ring_relay(c, stage):
        place, part, me, devs = ring(c, stage)
        down, up = (me + 3) % 4, (me + 1) % 4
        ring_copy(c, stage, 0, place(down), devs[0]).wait_recv()
        ring_copy(c, stage, 2, part(down, 0), devs[0]).start()
        ring_copy(c, stage, 1, place(up), devs[1]).wait_recv()
        ring_copy(c, stage, 3, part(up, 1), devs[1]).start()
        return place(down), place(up)

    def ring_end(c, stage):
        place, part, me, devs = ring(c, stage)
        far = (me + 2) % 4
        ring_copy(c, stage, 2, part(far, 0), devs[0]).wait_recv()
        ring_copy(c, stage, 3, part(far, 1), devs[1]).wait_recv()
        return place(far)

    def core_copy(c, i):
        place, part, me, devs = ring(c, 1)
        ref = place((me + i) % 4)
        return remote(ref, ref, core_s.at[c, i], core_r.at[c, i], other)

    def core_arrival(c, i):
        along_y = c not in Y_FIRST
        p = ((y if along_y else x) + i) % 4
        ref = wb.at[c, 1 - core, :, p] if along_y else wb.at[c, 1 - core, p]
        return remote(ref, ref, core_s.at[c, i], core_r.at[c, i], other)

    for c in range(GROUPS):
        ring_start(c, 0)
    for g in ORDER:
        rows(2, g)
        columns(2, g, 0)
    for c in range(GROUPS):
        ring_relay(c, 0)
    for c in range(GROUPS):
        ring_end(c, 0)
        ring_start(c, 1)
        core_copy(c, 0).start()
    for g in RELAYED:
        pass_rows(2, g)
        pass_columns(2, g, (0,))
    for c in range(GROUPS):
        if c in (0, 2):
            all_rows_then_columns(c // 2)
        ring_relay(c, 1)
        core_copy(c, 1).start()
        core_copy(c, 3).start()
    for c in range(GROUPS):
        ring_end(c, 1)
        core_copy(c, 2).start()
        for i in range(4):
            core_arrival(c, i).wait_recv()
        total = jnp.zeros((TOK, PER * HD), F32)
        for s in range(SLABS):
            w = wb[c, s // 4, s % 4].reshape(PER * HD, SLABW)
            total += nt(grads[:, s * SLABW:(s + 1) * SLABW], w)
        for i in range(PER):
            dn[c * PER + i, OWN] = total[:, i * HD:(i + 1) * HD].astype(BF)
        rows(3, c)
        columns(3, c, 0)
        if c < 2:
            for g in RELAYED:
                pass_columns(c, g, (-1, 1))
        if c == 1:
            all_rows_then_columns(2)

    lane = lax.broadcasted_iota(jnp.int32, (1, CELLS), 1)
    slot, token = lane // TOK, lane % TOK
    dr, dc = slot % 3 - 1, slot // 3 - 1
    row = (th + dr) * 8 + (token // 8) % 8
    col = (tw + dc) * 8 + token % 8
    limit_rows, limit_cols = 128 - pad_ref[0], 128 - pad_ref[1]
    key_ok = (row >= 0) & (row < limit_rows) & (col >= 0) & (col < limit_cols)
    query_ok = (row >= 0) & (row < 128) & (col >= 0) & (col < 128)
    key_bias = jnp.where(key_ok, 0.0, MASKED)
    query_bias = jnp.where(query_ok, 0.0, MASKED)
    far_rows, far_cols = jnp.abs(dr), jnp.abs(dc)

    def window(h, bias):
        inside = (far_rows <= ext_ref[0, h]) & (far_cols <= ext_ref[1, h])
        return jnp.where(inside, bias, MASKED)

    lane_of = lax.broadcasted_iota(jnp.int32, (TOK, TOK), 1)

    def forward(g, found):
        for i in range(PER):
            h = g * PER + i
            p = place_ref[h]
            s = nt(natural[2, h], kn[p].reshape(CELLS, HD)) * FACTOR + window(h, key_bias)
            top = jnp.max(s, axis=1, keepdims=True)
            e = jnp.exp(s - top)
            summed = jnp.sum(e, axis=1, keepdims=True)
            w = (e * (1.0 / summed)).astype(BF)
            probs[h] = w
            o = nn(w, vn[p].reshape(CELLS, HD)).astype(BF)
            att[g, :, i * HD:(i + 1) * HD] = o
            correction = jnp.sum(o.astype(F32) * dn[h, OWN].astype(F32), axis=1, keepdims=True)
            found = jnp.where(lane_of == h, top + jnp.log(summed), found)
            found = jnp.where(lane_of == HEADS + h, correction, found)
        return found

    for g in RELAYED:
        pass_rows(3, g)
        pass_columns(3, g, (0,))
    for g in range(GROUPS):
        all_columns(0, g)
        all_columns(1, g)
    found = forward(0, jnp.zeros((TOK, TOK), F32))
    for g in RELAYED:
        pass_columns(2, g, (-1, 1))
    rows_then_columns(3, 0)
    rows_then_columns(3, 1)
    found = forward(1, found)
    rows_then_columns(3, 2)
    rows_then_columns(3, 3)
    found = forward(2, found)
    found = forward(3, found)
    own_stats[...] = found
    stats[OWN] = found.T[0:2 * HEADS]

    around = [(a, b) for a in (-1, 0, 1) for b in (-1, 0, 1) if (a, b) != (0, 0)]

    def stat(a, b):
        j = (b + 1) * 3 + a + 1
        return remote(stats.at[OWN], stats.at[j], stat_s.at[j], stat_r.at[j], tile(-a, -b))

    for a, b in around:
        stat(a, b).start()

    for g in RELAYED:
        pass_columns(3, g, (-1, 1))

    for s in range(SLABS):
        total = jnp.zeros((TOK, SLABW), F32)
        for c in range(GROUPS):
            total += nn(att[c], wb[c, s // 4, s % 4].reshape(PER * HD, SLABW))
        out_ref[:, s * SLABW:(s + 1) * SLABW] = total.astype(BF)

    def query_part(g, carry):
        for i in range(PER):
            h = g * PER + i
            correction = jnp.sum(jnp.where(lane_of == HEADS + h, own_stats[...], 0.0), axis=1, keepdims=True)
            p = place_ref[h]
            dp = nt(dn[h, OWN], vn[p].reshape(CELLS, HD))
            ds = (probs[h].astype(F32) * (dp - correction)).astype(BF)
            dq = nn(ds, kn[p].reshape(CELLS, HD)) * FACTOR
            dq_ref[:, pl.ds(pl.multiple_of(h * HD, HD), HD)] = dq.astype(BF)
        return carry

    lax.fori_loop(0, GROUPS, query_part, 0)

    for a, b in around:
        stat(a, b).wait_recv()
    cell = lax.broadcasted_iota(jnp.int32, (TOK, 1), 0)
    own_ok = (th * 8 + (cell // 8) % 8 < limit_rows) & (tw * 8 + cell % 8 < limit_cols)

    for g in range(GROUPS):
        all_columns(2, g)

    def key_part(g, carry):
        all_columns(3, g)
        for i in range(PER):
            h = g * PER + i
            totals = jnp.concatenate([stats[j, pl.ds(h, 1)] for j in range(9)], axis=1)
            corrections = jnp.concatenate([stats[j, pl.ds(HEADS + h, 1)] for j in range(9)], axis=1)
            shift = window(h, query_bias) - totals
            qs = qn[place_ref[h]].reshape(CELLS, HD)
            ds_near = dn[h].reshape(CELLS, HD)
            w = jnp.exp(nt(natural[0, h], qs) * FACTOR + shift)
            dp = nt(natural[1, h], ds_near)
            ds = (w * (dp - corrections)).astype(BF)
            dk = jnp.where(own_ok, nn(ds, qs) * FACTOR, 0.0)
            dv = jnp.where(own_ok, nn(w.astype(BF), ds_near), 0.0)
            at_h = pl.ds(pl.multiple_of(h * HD, HD), HD)
            dk_ref[:, at_h] = dk.astype(BF)
            dv_ref[:, at_h] = dv.astype(BF)
        return carry

    lax.fori_loop(0, GROUPS, key_part, 0)

    for i in range(1, 8):
        remote(padded.at[0], pieces.at[0], piece_s.at[i - 1], piece_r.at[i - 1], near_xc[i - 1]).wait_send()
        remote(block, z_place(z), z_s.at[i - 1], z_r.at[i - 1], near_z[i - 1]).wait_send()
    for c in range(GROUPS):
        for stage in range(2):
            place, part, me, devs = ring(c, stage)
            for i in range(2):
                ring_copy(c, stage, i, place(me), devs[i]).wait_send()
                ring_copy(c, stage, 2 + i, part(me, 0), devs[i]).wait_send()
        for i in range(4):
            core_copy(c, i).wait_send()
    for number in range(4):
        for g in range(GROUPS):
            halo(number, g, 3, OWN, north).wait_send()
            halo(number, g, 5, OWN, north).wait_send()
            for edge, slots in ((last_col, (0, 1, 2)), (first_col, (6, 7, 8))):
                @pl.when(jnp.logical_not(edge))
                def _():
                    for slot in slots:
                        halo(number, g, slot, OWN, north).wait_send()
            if g in RELAYED:
                @pl.when(first_row | last_row)
                def _():
                    row_pass(number, g, 3, north).wait_send()

                @pl.when(first_col | last_col)
                def _():
                    for dr in (-1, 0, 1):
                        col_pass(number, g, dr, 1 + dr, north).wait_send()
    for a, b in around:
        stat(a, b).wait_send()


def run(number, q, k, v, out_grad, pieces, extent, pad):
    hbm = pl.BlockSpec(memory_space=pl.ANY)
    smem = pl.BlockSpec(memory_space=pltpu.SMEM)
    vmem = pl.BlockSpec(memory_space=pltpu.VMEM)
    near = pltpu.VMEM((HEADS, 9, TOK, HD), BF)
    dma = pltpu.SemaphoreType.DMA
    return pl.pallas_call(
        functools.partial(kernel, SIZES[number]),
        out_shape=(
            jax.ShapeDtypeStruct((TOK, D), BF),
            jax.ShapeDtypeStruct((TOK, E), BF),
            jax.ShapeDtypeStruct((TOK, E), BF),
            jax.ShapeDtypeStruct((TOK, E), BF),
        ),
        in_specs=[smem, smem, hbm, hbm, hbm, hbm, vmem],
        out_specs=(vmem, vmem, vmem, vmem),
        scratch_shapes=[
            near, near, near, near,
            pltpu.VMEM((GROUPS, 2, 4, 4, 96, SLABW), BF),
            pltpu.VMEM((TOK, D), BF),
            pltpu.VMEM((8, 16, SLABW), BF),
            pltpu.VMEM((48, SLABW), BF),
            pltpu.VMEM((GROUPS, TOK, PER * HD), BF),
            pltpu.VMEM((HEADS, TOK, CELLS), BF),
            pltpu.VMEM((TOK, TOK), F32),
            pltpu.VMEM((9, 2 * HEADS, TOK), F32),
            dma((4, HEADS)),
            dma((7,)), dma((7,)), dma((7,)), dma((7,)),
            dma((GROUPS, 2, 4)), dma((GROUPS, 2, 4)),
            dma((GROUPS, 4)), dma((GROUPS, 4)),
            dma((4, GROUPS, 9)), dma((4, GROUPS, 9)),
            dma((9,)), dma((9,)),
            pltpu.VMEM((4, 2, PER, TOK, HD), BF),
            pltpu.VMEM((4, 2, 3, PER, TOK, HD), BF),
            pltpu.VMEM((3, HEADS, TOK, HD), BF),
            pltpu.SMEM((HEADS,), jnp.int32),
            pltpu.VMEM((8, 16, SLABW), BF),
            dma((4, 2)), dma((4, 2)), dma((4, 2, 3)), dma((4, 2, 3)),
        ],
        compiler_params=pltpu.CompilerParams(
            collective_id=number, has_side_effects=True, vmem_limit_bytes=60 * 1024 * 1024),
        cost_estimate=pl.CostEstimate(flops=7 * 10**9, bytes_accessed=6 * 10**6, transcendentals=4 * 10**6),
    )(extent, pad, q, k, v, out_grad, pieces)


def choose(ext_ref, number_ref):
    both = rows_only = cols_only = jnp.int32(0)
    for h in range(HEADS):
        in_rows, in_cols = ext_ref[0, h], ext_ref[1, h]
        both += in_rows * in_cols
        rows_only += in_rows * (1 - in_cols)
        cols_only += in_cols * (1 - in_rows)
    number = jnp.int32(len(SIZES) - 1)
    for i in reversed(range(len(SIZES) - 1)):
        n_rows, n_cols, n_both = SIZES[i]
        beyond = jnp.maximum(rows_only - (n_rows - n_both), 0) + jnp.maximum(cols_only - (n_cols - n_both), 0)
        number = jnp.where(beyond + both <= n_both, i, number)
    number_ref[0] = number


def choice(extent):
    smem = pl.BlockSpec(memory_space=pltpu.SMEM)
    number = pl.pallas_call(
        choose,
        out_shape=jax.ShapeDtypeStruct((1,), jnp.int32),
        in_specs=[smem],
        out_specs=smem,
    )(extent)
    return number[0]


def on_device(q, k, v, out_grad, out_weight, extent, pad):
    shape = q.shape
    flat = lambda a: a.reshape(TOK, a.shape[-1])
    pieces = out_weight.reshape(6, SLABS, SLABW).transpose(1, 0, 2)
    out, dq, dk, dv = lax.switch(
        choice(extent), [functools.partial(run, i) for i in range(len(SIZES))],
        flat(q), flat(k), flat(v), flat(out_grad), pieces, extent, pad)
    return (out.reshape(out_grad.shape), dq.reshape(shape), dk.reshape(shape), dv.reshape(shape))


def solution(mesh):
    cells = P(None, "th", "tw", None)
    return jax.shard_map(
        on_device,
        mesh=mesh,
        in_specs=(cells, cells, cells, cells, P(("th", "tw"), None), P(), P()),
        out_specs=(cells, cells, cells, cells),
        check_vma=False,
    )
```

```python
import functools

import jax
import jax.numpy as jnp
from jax import lax
from jax.experimental import pallas as pl
from jax.experimental.pallas import tpu as pltpu
from jax.sharding import PartitionSpec as P

MESH = pl.DeviceIdType.MESH
HEADS, HD, TOK = 12, 128, 128
GROUPS, PER = 4, 3
D, E = 3072, 1536
SLABS = 8
SLABW = D // SLABS
OWN = 4
RELAYED = (2, 3)
ORDER = (2, 3, 0, 1)
Y_FIRST = (1, 3)
CELLS = 9 * TOK
SIZES = ((9, 8, 5), (12, 12, 12))
MASKED = -1e30
FACTOR = HD ** (-0.5)
BF, F32 = jnp.bfloat16, jnp.float32


def nt(a, b):
    return lax.dot_general(a, b, (((1,), (1,)), ((), ())), preferred_element_type=F32)


def nn(a, b):
    return jnp.dot(a, b, preferred_element_type=F32)


def kernel(
    sizes, ext_ref, pad_ref, q_hbm, k_hbm, v_hbm, g_hbm, w_ref,
    out_ref, dq_ref, dk_ref, dv_ref,
    qn, kn, vn, dn, wb, grads, pieces, block, att, probs, own_stats, stats,
    load_sem, piece_s, piece_r, z_s, z_r, ring_s, ring_r, core_s, core_r, halo_s, halo_r, stat_s, stat_r,
    row_relay, col_relay, natural, place_ref, padded, row_rs, row_rr, col_rs, col_rr,
):
    th, tw = lax.axis_index("th"), lax.axis_index("tw")
    zh, y = th // 4, th % 4
    zl, x, core = tw // 8, (tw // 2) % 4, tw % 2
    z = zh * 2 + zl

    def at(zz, yy, xx, cc):
        return ((zz // 2) * 4 + yy, (zz % 2) * 8 + xx * 2 + cc)

    def tile(dr, dc):
        return ((th + dr + 16) % 16, (tw + dc + 16) % 16)

    north, south, west, east = tile(-1, 0), tile(1, 0), tile(0, -1), tile(0, 1)
    y_up, y_down = (y + 1) % 4, (y + 3) % 4
    x_up, x_down = (x + 1) % 4, (x + 3) % 4
    near_xc = [at(z, y, ((x * 2 + core + i) % 8) // 2, (core + i) % 2) for i in range(1, 8)]
    near_z = [at((z + i) % 8, y, x, core) for i in range(1, 8)]
    near_y = [at(z, y_up, x, core), at(z, y_down, x, core)]

    def remote(src, dst, send, recv, device):
        return pltpu.make_async_remote_copy(
            src_ref=src, dst_ref=dst, send_sem=send, recv_sem=recv,
            device_id=device, device_id_type=MESH,
        )

    barrier = pltpu.get_barrier_semaphore()
    corners = [tile(-1, -1), tile(-1, 1), tile(1, -1), tile(1, 1)]
    greeted = [north, south, west, east] + near_xc + near_z + near_y + corners
    for target in greeted:
        pl.semaphore_signal(barrier, inc=1, device_id=target, device_id_type=MESH)
    loads = []
    for number, hbm in enumerate((k_hbm, v_hbm, q_hbm)):
        for h in range(HEADS):
            loads.append(pltpu.make_async_copy(
                hbm.at[:, pl.ds(h * HD, HD)], natural.at[number, h], load_sem.at[number, h]))
    loads.append(pltpu.make_async_copy(g_hbm, grads, load_sem.at[3, 0]))
    mine = x * 2 + core
    slab = core * 4 + x
    for copy in loads:
        copy.start()
    padded[...] = jnp.zeros_like(padded)
    padded[:, 0:6, :] = w_ref[...]
    own_piece = pltpu.make_async_copy(padded.at[slab], pieces.at[mine], load_sem.at[3, 1])
    own_piece.start()

    n_rows, n_cols, n_both = sizes
    row_only, col_only = n_rows - n_both, n_cols - n_both
    none_left = HEADS - n_rows - col_only
    in_rows = [ext_ref[0, h] for h in range(HEADS)]
    in_cols = [ext_ref[1, h] for h in range(HEADS)]
    used = [jnp.int32(0)] * 4
    places = [jnp.int32(0)] * HEADS
    starts = (0, row_only, n_rows, n_rows + col_only)
    room = (row_only, n_both, col_only, none_left)
    for wanted_rows, wanted_cols, pools in ((1, 1, (1,)), (1, 0, (0, 1)), (0, 1, (2, 1)), (0, 0, (3, 0, 2, 1))):
        for h in range(HEADS):
            open_now = (in_rows[h] == wanted_rows) & (in_cols[h] == wanted_cols)
            for pool in pools:
                take = open_now if pool == pools[-1] else open_now & (used[pool] < room[pool])
                places[h] = jnp.where(take, starts[pool] + used[pool], places[h])
                used[pool] = used[pool] + take.astype(jnp.int32)
                open_now = open_now & jnp.logical_not(take)
    for h in range(HEADS):
        place_ref[h] = places[h]
    heads_at = [
        sum(jnp.where(places[h] == p, h, 0) for h in range(HEADS)) for p in range(HEADS)]

    ranges = {}
    for j in (3, 5):
        ranges[j] = (0, n_rows)
    for j in (1, 7):
        ranges[j] = (row_only, n_rows + col_only)
    for j in (0, 2, 6, 8):
        ranges[j] = (row_only, n_rows)
    for near in (kn, vn, qn):
        for j, (low, high) in ranges.items():
            if low:
                near[0:low, j] = jnp.zeros((low, TOK, HD), BF)
            if high < HEADS:
                near[high:HEADS, j] = jnp.zeros((HEADS - high, TOK, HD), BF)
    for edge, slots in ((tw == 0, (0, 1, 2)), (tw == 15, (6, 7, 8))):
        @pl.when(edge)
        def _():
            for near in (kn, vn, qn, dn):
                for j in slots:
                    near[:, j] = jnp.zeros((HEADS, TOK, HD), BF)
    for copy in loads:
        copy.wait()
    own_piece.wait()
    for p in range(HEADS):
        for number, near in enumerate((kn, vn, qn)):
            near[p, OWN] = natural[number, heads_at[p]]
    pl.semaphore_wait(barrier, len(greeted))

    nears = (kn, vn, qn, dn)

    def span(number, g, slot):
        if number == 3:
            return g * PER, PER
        low, high = ranges[slot]
        first = low + (high - low) * g // GROUPS
        return first, low + (high - low) * (g + 1) // GROUPS - first

    def halo(number, g, slot, source, device):
        near = nears[number]
        heads = pl.ds(*span(number, g, slot))
        return remote(near.at[heads, source], near.at[heads, slot],
                      halo_s.at[number, g, slot], halo_r.at[number, g, slot], device)

    first_row, last_row = y == 0, y == 3
    first_col, last_col = tw == 0, tw == 15
    cross_east, cross_west = tw == 7, tw == 8

    def via(number, g, slot, source, space, send, recv, device):
        first, count = span(number, g, slot)
        return remote(nears[number].at[pl.ds(first, count), source], space.at[pl.ds(0, count)], send, recv, device)

    def rows(number, g):
        if g in RELAYED:
            i = g - RELAYED[0]
            for slot, crossing, straight, device in (
                (3, last_row, south, tile(-3, 0)), (5, first_row, north, tile(3, 0))):
                @pl.when(crossing)
                def _():
                    via(number, g, slot, OWN, row_relay.at[number, i], halo_s.at[number, g, slot],
                        row_rr.at[number, i], device).start()

                @pl.when(jnp.logical_not(crossing))
                def _():
                    halo(number, g, slot, OWN, straight).start()
        else:
            halo(number, g, 3, OWN, south).start()
            halo(number, g, 5, OWN, north).start()

    def row_pass(number, g, slot, device):
        i = g - RELAYED[0]
        first, count = span(number, g, slot)
        return remote(row_relay.at[number, i, pl.ds(0, count)], nears[number].at[pl.ds(first, count), slot],
                      row_rs.at[number, i], halo_r.at[number, g, slot], device)

    def pass_rows(number, g):
        if g not in RELAYED:
            return
        i = g - RELAYED[0]
        for slot, crossing, device in ((3, first_row, tile(4, 0)), (5, last_row, tile(-4, 0))):
            @pl.when(crossing)
            def _():
                via(number, g, slot, OWN, row_relay.at[number, i], row_rs.at[number, i],
                    row_rr.at[number, i], north).wait_recv()
                row_pass(number, g, slot, device).start()

    def columns(number, g, dr):
        for slot, crossing, edge, straight, device in (
            (1 + dr, cross_east, last_col, east, tile(0, -7)),
            (7 + dr, cross_west, first_col, west, tile(0, 7))):
            if g in RELAYED:
                i = g - RELAYED[0]

                @pl.when(crossing)
                def _():
                    via(number, g, slot, OWN + dr, col_relay.at[number, i, dr + 1],
                        halo_s.at[number, g, slot], col_rr.at[number, i, dr + 1], device).start()

                @pl.when(jnp.logical_not(crossing | edge))
                def _():
                    halo(number, g, slot, OWN + dr, straight).start()
            else:
                @pl.when(jnp.logical_not(edge))
                def _():
                    halo(number, g, slot, OWN + dr, straight).start()

    def col_pass(number, g, dr, slot, device):
        i = g - RELAYED[0]
        first, count = span(number, g, slot)
        return remote(col_relay.at[number, i, dr + 1, pl.ds(0, count)], nears[number].at[pl.ds(first, count), slot],
                      col_rs.at[number, i, dr + 1], halo_r.at[number, g, slot], device)

    def pass_columns(number, g, drs=(0, -1, 1)):
        if g not in RELAYED:
            return
        i = g - RELAYED[0]
        for base, edge, device in ((1, first_col, tile(0, 8)), (7, last_col, tile(0, -8))):
            @pl.when(edge)
            def _():
                for dr in drs:
                    via(number, g, base + dr, OWN, col_relay.at[number, i, dr + 1], col_rs.at[number, i, dr + 1],
                        col_rr.at[number, i, dr + 1], north).wait_recv()
                    col_pass(number, g, dr, base + dr, device).start()

    def arrived(number, g, slot):
        halo(number, g, slot, OWN, north).wait_recv()

    def rows_then_columns(number, g):
        arrived(number, g, 3)
        columns(number, g, -1)
        arrived(number, g, 5)
        columns(number, g, 1)

    def all_rows_then_columns(number):
        for g in range(GROUPS):
            arrived(number, g, 3)
            arrived(number, g, 5)
        for g in ORDER:
            columns(number, g, -1)
            columns(number, g, 1)

    def all_columns(number, g):
        @pl.when(jnp.logical_not(first_col))
        def _():
            for slot in (0, 1, 2):
                arrived(number, g, slot)

        @pl.when(jnp.logical_not(last_col))
        def _():
            for slot in (6, 7, 8):
                arrived(number, g, slot)

    for i in range(1, 8):
        t = (mine + i) % 8
        remote(padded.at[(t % 2) * 4 + t // 2], pieces.at[mine], piece_s.at[i - 1], piece_r.at[i - 1],
               near_xc[i - 1]).start()
    for number in (0, 1):
        for g in ORDER:
            rows(number, g)
            columns(number, g, 0)
    for i in range(1, 8):
        remote(padded.at[0], pieces.at[(mine + 8 - i) % 8], piece_s.at[i - 1], piece_r.at[i - 1],
               near_xc[i - 1]).wait_recv()
    block[...] = jnp.concatenate(
        [pieces[t].astype(F32)[0:6] for t in range(8)], axis=0).astype(BF)

    def z_place(zz):
        return wb.at[zz // 2, core, x, y, pl.ds((zz % 2) * 48, 48)]

    own_place = pltpu.make_async_copy(block, z_place(z), load_sem.at[3, 2])
    own_place.start()
    for i in range(1, 8):
        remote(block, z_place(z), z_s.at[i - 1], z_r.at[i - 1], near_z[i - 1]).start()
    own_place.wait()
    for number in (0, 1):
        for g in RELAYED:
            pass_rows(number, g)
            pass_columns(number, g, (0,))
    for i in range(1, 8):
        remote(block, z_place((z + 8 - i) % 8), z_s.at[i - 1], z_r.at[i - 1], near_z[i - 1]).wait_recv()

    y_dev = (at(z, y_up, x, core), at(z, y_down, x, core))
    x_dev = (at(z, y, x_up, core), at(z, y, x_down, core))
    other = at(z, y, x, 1 - core)
    half = lambda i: pl.ds(i * 2, 2)

    def ring(c, stage):
        along_y = (c in Y_FIRST) == (stage == 0)
        if along_y:
            me, devs = y, y_dev
            if stage == 0:
                place = lambda p: wb.at[c, core, x, p]
                part = lambda p, i: wb.at[c, core, x, p, pl.ds(i * 48, 48)]
            else:
                place = lambda p: wb.at[c, core, :, p]
                part = lambda p, i: wb.at[c, core, half(i), p]
        else:
            me, devs = x, x_dev
            if stage == 0:
                place = lambda p: wb.at[c, core, p, y]
                part = lambda p, i: wb.at[c, core, p, y, pl.ds(i * 48, 48)]
            else:
                place = lambda p: wb.at[c, core, p]
                part = lambda p, i: wb.at[c, core, p, half(i)]
        return place, part, me, devs

    def ring_copy(c, stage, i, ref, device):
        return remote(ref, ref, ring_s.at[c, stage, i], ring_r.at[c, stage, i], device)

    def ring_start(c, stage):
        place, part, me, devs = ring(c, stage)
        ring_copy(c, stage, 0, place(me), devs[0]).start()
        ring_copy(c, stage, 1, place(me), devs[1]).start()

    def ring_relay(c, stage):
        place, part, me, devs = ring(c, stage)
        down, up = (me + 3) % 4, (me + 1) % 4
        ring_copy(c, stage, 0, place(down), devs[0]).wait_recv()
        ring_copy(c, stage, 2, part(down, 0), devs[0]).start()
        ring_copy(c, stage, 1, place(up), devs[1]).wait_recv()
        ring_copy(c, stage, 3, part(up, 1), devs[1]).start()
        return place(down), place(up)

    def ring_end(c, stage):
        place, part, me, devs = ring(c, stage)
        far = (me + 2) % 4
        ring_copy(c, stage, 2, part(far, 0), devs[0]).wait_recv()
        ring_copy(c, stage, 3, part(far, 1), devs[1]).wait_recv()
        return place(far)

    def core_copy(c, i):
        place, part, me, devs = ring(c, 1)
        ref = place((me + i) % 4)
        return remote(ref, ref, core_s.at[c, i], core_r.at[c, i], other)

    def core_arrival(c, i):
        along_y = c not in Y_FIRST
        p = ((y if along_y else x) + i) % 4
        ref = wb.at[c, 1 - core, :, p] if along_y else wb.at[c, 1 - core, p]
        return remote(ref, ref, core_s.at[c, i], core_r.at[c, i], other)

    for c in range(GROUPS):
        ring_start(c, 0)
    for g in ORDER:
        rows(2, g)
        columns(2, g, 0)
    for c in range(GROUPS):
        ring_relay(c, 0)
    for c in range(GROUPS):
        ring_end(c, 0)
        ring_start(c, 1)
        core_copy(c, 0).start()
    for g in RELAYED:
        pass_rows(2, g)
        pass_columns(2, g, (0,))
    for c in range(GROUPS):
        if c in (0, 2):
            all_rows_then_columns(c // 2)
        ring_relay(c, 1)
        core_copy(c, 1).start()
        core_copy(c, 3).start()
    for c in range(GROUPS):
        ring_end(c, 1)
        core_copy(c, 2).start()
        for i in range(4):
            core_arrival(c, i).wait_recv()
        total = jnp.zeros((TOK, PER * HD), F32)
        for s in range(SLABS):
            w = wb[c, s // 4, s % 4].reshape(PER * HD, SLABW)
            total += nt(grads[:, s * SLABW:(s + 1) * SLABW], w)
        for i in range(PER):
            dn[c * PER + i, OWN] = total[:, i * HD:(i + 1) * HD].astype(BF)
        rows(3, c)
        columns(3, c, 0)
        if c < 2:
            for g in RELAYED:
                pass_columns(c, g, (-1, 1))
        if c == 1:
            all_rows_then_columns(2)

    lane = lax.broadcasted_iota(jnp.int32, (1, CELLS), 1)
    slot, token = lane // TOK, lane % TOK
    dr, dc = slot % 3 - 1, slot // 3 - 1
    row = (th + dr) * 8 + (token // 8) % 8
    col = (tw + dc) * 8 + token % 8
    limit_rows, limit_cols = 128 - pad_ref[0], 128 - pad_ref[1]
    key_ok = (row >= 0) & (row < limit_rows) & (col >= 0) & (col < limit_cols)
    query_ok = (row >= 0) & (row < 128) & (col >= 0) & (col < 128)
    key_bias = jnp.where(key_ok, 0.0, MASKED)
    query_bias = jnp.where(query_ok, 0.0, MASKED)
    far_rows, far_cols = jnp.abs(dr), jnp.abs(dc)

    def window(h, bias):
        inside = (far_rows <= ext_ref[0, h]) & (far_cols <= ext_ref[1, h])
        return jnp.where(inside, bias, MASKED)

    lane_of = lax.broadcasted_iota(jnp.int32, (TOK, TOK), 1)

    def forward(g, found):
        for i in range(PER):
            h = g * PER + i
            p = place_ref[h]
            s = nt(natural[2, h], kn[p].reshape(CELLS, HD)) * FACTOR + window(h, key_bias)
            top = jnp.max(s, axis=1, keepdims=True)
            e = jnp.exp(s - top)
            summed = jnp.sum(e, axis=1, keepdims=True)
            w = (e * (1.0 / summed)).astype(BF)
            probs[h] = w
            o = nn(w, vn[p].reshape(CELLS, HD)).astype(BF)
            att[g, :, i * HD:(i + 1) * HD] = o
            correction = jnp.sum(o.astype(F32) * dn[h, OWN].astype(F32), axis=1, keepdims=True)
            found = jnp.where(lane_of == h, top + jnp.log(summed), found)
            found = jnp.where(lane_of == HEADS + h, correction, found)
        return found

    for g in RELAYED:
        pass_rows(3, g)
        pass_columns(3, g, (0,))
    for g in range(GROUPS):
        all_columns(0, g)
        all_columns(1, g)
    found = forward(0, jnp.zeros((TOK, TOK), F32))
    for g in RELAYED:
        pass_columns(2, g, (-1, 1))
    rows_then_columns(3, 0)
    rows_then_columns(3, 1)
    found = forward(1, found)
    rows_then_columns(3, 2)
    rows_then_columns(3, 3)
    found = forward(2, found)
    found = forward(3, found)
    own_stats[...] = found
    stats[OWN] = found.T[0:2 * HEADS]

    around = [(a, b) for a in (-1, 0, 1) for b in (-1, 0, 1) if (a, b) != (0, 0)]

    def stat(a, b):
        j = (b + 1) * 3 + a + 1
        return remote(stats.at[OWN], stats.at[j], stat_s.at[j], stat_r.at[j], tile(-a, -b))

    for a, b in around:
        stat(a, b).start()

    for g in RELAYED:
        pass_columns(3, g, (-1, 1))

    for s in range(SLABS):
        total = jnp.zeros((TOK, SLABW), F32)
        for c in range(GROUPS):
            total += nn(att[c], wb[c, s // 4, s % 4].reshape(PER * HD, SLABW))
        out_ref[:, s * SLABW:(s + 1) * SLABW] = total.astype(BF)

    def query_part(g, carry):
        for i in range(PER):
            h = g * PER + i
            correction = jnp.sum(jnp.where(lane_of == HEADS + h, own_stats[...], 0.0), axis=1, keepdims=True)
            p = place_ref[h]
            dp = nt(dn[h, OWN], vn[p].reshape(CELLS, HD))
            ds = (probs[h].astype(F32) * (dp - correction)).astype(BF)
            dq = nn(ds, kn[p].reshape(CELLS, HD)) * FACTOR
            dq_ref[:, pl.ds(pl.multiple_of(h * HD, HD), HD)] = dq.astype(BF)
        return carry

    lax.fori_loop(0, GROUPS, query_part, 0)

    for a, b in around:
        stat(a, b).wait_recv()
    cell = lax.broadcasted_iota(jnp.int32, (TOK, 1), 0)
    own_ok = (th * 8 + (cell // 8) % 8 < limit_rows) & (tw * 8 + cell % 8 < limit_cols)

    for g in range(GROUPS):
        all_columns(2, g)

    def key_part(g, carry):
        all_columns(3, g)
        for i in range(PER):
            h = g * PER + i
            totals = jnp.concatenate([stats[j, pl.ds(h, 1)] for j in range(9)], axis=1)
            corrections = jnp.concatenate([stats[j, pl.ds(HEADS + h, 1)] for j in range(9)], axis=1)
            shift = window(h, query_bias) - totals
            qs = qn[place_ref[h]].reshape(CELLS, HD)
            ds_near = dn[h].reshape(CELLS, HD)
            w = jnp.exp(nt(natural[0, h], qs) * FACTOR + shift)
            dp = nt(natural[1, h], ds_near)
            ds = (w * (dp - corrections)).astype(BF)
            dk = jnp.where(own_ok, nn(ds, qs) * FACTOR, 0.0)
            dv = jnp.where(own_ok, nn(w.astype(BF), ds_near), 0.0)
            at_h = pl.ds(pl.multiple_of(h * HD, HD), HD)
            dk_ref[:, at_h] = dk.astype(BF)
            dv_ref[:, at_h] = dv.astype(BF)
        return carry

    lax.fori_loop(0, GROUPS, key_part, 0)

    for i in range(1, 8):
        remote(padded.at[0], pieces.at[0], piece_s.at[i - 1], piece_r.at[i - 1], near_xc[i - 1]).wait_send()
        remote(block, z_place(z), z_s.at[i - 1], z_r.at[i - 1], near_z[i - 1]).wait_send()
    for c in range(GROUPS):
        for stage in range(2):
            place, part, me, devs = ring(c, stage)
            for i in range(2):
                ring_copy(c, stage, i, place(me), devs[i]).wait_send()
                ring_copy(c, stage, 2 + i, part(me, 0), devs[i]).wait_send()
        for i in range(4):
            core_copy(c, i).wait_send()
    for number in range(4):
        for g in range(GROUPS):
            halo(number, g, 3, OWN, north).wait_send()
            halo(number, g, 5, OWN, north).wait_send()
            for edge, slots in ((last_col, (0, 1, 2)), (first_col, (6, 7, 8))):
                @pl.when(jnp.logical_not(edge))
                def _():
                    for slot in slots:
                        halo(number, g, slot, OWN, north).wait_send()
            if g in RELAYED:
                @pl.when(first_row | last_row)
                def _():
                    row_pass(number, g, 3, north).wait_send()

                @pl.when(first_col | last_col)
                def _():
                    for dr in (-1, 0, 1):
                        col_pass(number, g, dr, 1 + dr, north).wait_send()
    for a, b in around:
        stat(a, b).wait_send()


def run(number, q, k, v, out_grad, pieces, extent, pad):
    hbm = pl.BlockSpec(memory_space=pl.ANY)
    smem = pl.BlockSpec(memory_space=pltpu.SMEM)
    vmem = pl.BlockSpec(memory_space=pltpu.VMEM)
    near = pltpu.VMEM((HEADS, 9, TOK, HD), BF)
    dma = pltpu.SemaphoreType.DMA
    return pl.pallas_call(
        functools.partial(kernel, SIZES[number]),
        out_shape=(
            jax.ShapeDtypeStruct((TOK, D), BF),
            jax.ShapeDtypeStruct((TOK, E), BF),
            jax.ShapeDtypeStruct((TOK, E), BF),
            jax.ShapeDtypeStruct((TOK, E), BF),
        ),
        in_specs=[smem, smem, hbm, hbm, hbm, hbm, vmem],
        out_specs=(vmem, vmem, vmem, vmem),
        scratch_shapes=[
            near, near, near, near,
            pltpu.VMEM((GROUPS, 2, 4, 4, 96, SLABW), BF),
            pltpu.VMEM((TOK, D), BF),
            pltpu.VMEM((8, 16, SLABW), BF),
            pltpu.VMEM((48, SLABW), BF),
            pltpu.VMEM((GROUPS, TOK, PER * HD), BF),
            pltpu.VMEM((HEADS, TOK, CELLS), BF),
            pltpu.VMEM((TOK, TOK), F32),
            pltpu.VMEM((9, 2 * HEADS, TOK), F32),
            dma((4, HEADS)),
            dma((7,)), dma((7,)), dma((7,)), dma((7,)),
            dma((GROUPS, 2, 4)), dma((GROUPS, 2, 4)),
            dma((GROUPS, 4)), dma((GROUPS, 4)),
            dma((4, GROUPS, 9)), dma((4, GROUPS, 9)),
            dma((9,)), dma((9,)),
            pltpu.VMEM((4, 2, PER, TOK, HD), BF),
            pltpu.VMEM((4, 2, 3, PER, TOK, HD), BF),
            pltpu.VMEM((3, HEADS, TOK, HD), BF),
            pltpu.SMEM((HEADS,), jnp.int32),
            pltpu.VMEM((8, 16, SLABW), BF),
            dma((4, 2)), dma((4, 2)), dma((4, 2, 3)), dma((4, 2, 3)),
        ],
        compiler_params=pltpu.CompilerParams(
            collective_id=number, has_side_effects=True, vmem_limit_bytes=60 * 1024 * 1024),
        cost_estimate=pl.CostEstimate(flops=7 * 10**9, bytes_accessed=6 * 10**6, transcendentals=4 * 10**6),
    )(extent, pad, q, k, v, out_grad, pieces)


def choose(ext_ref, number_ref):
    both = rows_only = cols_only = jnp.int32(0)
    for h in range(HEADS):
        in_rows, in_cols = ext_ref[0, h], ext_ref[1, h]
        both += in_rows * in_cols
        rows_only += in_rows * (1 - in_cols)
        cols_only += in_cols * (1 - in_rows)
    number = jnp.int32(len(SIZES) - 1)
    for i in reversed(range(len(SIZES) - 1)):
        n_rows, n_cols, n_both = SIZES[i]
        beyond = jnp.maximum(rows_only - (n_rows - n_both), 0) + jnp.maximum(cols_only - (n_cols - n_both), 0)
        number = jnp.where(beyond + both <= n_both, i, number)
    number_ref[0] = number


def choice(extent):
    smem = pl.BlockSpec(memory_space=pltpu.SMEM)
    number = pl.pallas_call(
        choose,
        out_shape=jax.ShapeDtypeStruct((1,), jnp.int32),
        in_specs=[smem],
        out_specs=smem,
    )(extent)
    return number[0]


def on_device(q, k, v, out_grad, out_weight, extent, pad):
    shape = q.shape
    flat = lambda a: a.reshape(TOK, a.shape[-1])
    pieces = out_weight.reshape(6, SLABS, SLABW).transpose(1, 0, 2)
    out, dq, dk, dv = lax.switch(
        choice(extent), [functools.partial(run, i) for i in range(len(SIZES))],
        flat(q), flat(k), flat(v), flat(out_grad), pieces, extent, pad)
    return (out.reshape(out_grad.shape), dq.reshape(shape), dk.reshape(shape), dv.reshape(shape))


def solution(mesh):
    cells = P(None, "th", "tw", None)
    return jax.shard_map(
        on_device,
        mesh=mesh,
        in_specs=(cells, cells, cells, cells, P(("th", "tw"), None), P(), P()),
        out_specs=(cells, cells, cells, cells),
        check_vma=False,
    )
```
